128 devices in a mesh: grp: 8 (over y, core), tp: 16 (over z, x).
Axes of the slice: x: 4, y: 4, z: 4, core: 2. Of those that a mesh axis runs over, the one named last changes fastest.
Arguments:
- prefill_x: bfloat16 [2048, 8192], P('grp', 'tp'), may hold values from -6 to 6
- span_index: int32 [8], replicated, may hold values from 0 to 7, as said below
- prefix_pages: int32 [8, 112], P('grp'), may hold values from 0 to 111, each once within a row
- prefix_cache: bfloat16 [8, 16, 1792, 256], P('grp', 'tp'), may hold values from -300 to 300, as said below
- decode_x: bfloat16 [2, 512, 8192], P(None, 'grp', 'tp'), may hold values from -6 to 6
- decode_len: int32 [8, 2, 32], P('grp'), may hold values from 1 to 512, 8192 in all within a row
- page_order: int32 [8, 2, 544], P('grp'), may hold values from 0 to 543, each once within a row
- assignment: int32 [8], replicated, may hold values from 0 to 7
- kv_cache: bfloat16 [8, 16, 8704, 256], P('grp', 'tp'), may hold values from -300 to 300
- w_query: bfloat16 [8192, 8192], P(None, 'tp'), may hold values from -0.0625 to 0.0625
- w_keyval: bfloat16 [8192, 2048], P(None, 'tp'), may hold values from -0.0625 to 0.0625
- w_out: bfloat16 [8192, 8192], P('tp'), may hold values from -0.0625 to 0.0625
Outputs:
- prefill_out: bfloat16 [2048, 8192], P('grp', 'tp')
- decode_out: bfloat16 [2, 512, 8192], P(None, 'grp', 'tp')
The draws below stay inside these ranges and needn't reach their ends.
Inputs may be any that keep to these rules, and one draw needn't show every extreme that they name: `span_index`: exactly 4 prompts are at span 8 - 1, and one prompt is at span 0. `prefix_pages`: each row holds every page number of its prefix pool once. `prefix_cache`: the pools h * 2 + m of one group are equal for every m < 2. `decode_len`: each row of 32 lengths sums to 8192, and its largest is 512. `page_order`: each row holds every page number of its pool once.
All inputs are finite; a program needn't handle non-finite values.
Results may differ from the reference program's by a relative error of at most 0.019.
Values may be sent and summed in bfloat16 or wider, within the bound.
A program may use at most 128 MiB of HBM per device.

```python
import math
import jax
import jax.numpy as jnp
import numpy as np
from jax import lax

D = 8192
HEADS = 64
KV_HEADS = 8
HEAD_DIM = 128
SPAN = 256
SPANS = 8
PAGE = 16
DECODE = 64
MEAN_LEN = 256
MOST_LEN = 512
MAX_PAGES = 32
PRE_POOL = 112
PROMPTS = 8
SPLIT = 2
DEC_DEV = 32
POOL_DEV = 544
N_GRP = 8
N_TP = 16


def spiked(key, shape):
    values = jax.random.normal(key, shape, jnp.float32)
    return jnp.clip(values, -300.0, 300.0)


def draw_kv_cache(key, part):
    key = jax.random.fold_in(key, 11)
    values = spiked(key, (N_GRP, N_TP, POOL_DEV * PAGE, 2 * HEAD_DIM))
    return values.astype(jnp.bfloat16)


def draw_prefix_cache(key, part):
    key = jax.random.fold_in(key, 13)
    values = spiked(key, (N_GRP, KV_HEADS, PRE_POOL * PAGE, 2 * HEAD_DIM))
    return jnp.repeat(values, N_TP // KV_HEADS, axis=1).astype(jnp.bfloat16)


def draw_span_index(key, part):
    key = jax.random.fold_in(key, 21)
    order = jax.random.permutation(jax.random.fold_in(key, 1), PROMPTS)
    others = jax.random.randint(jax.random.fold_in(key, 2), (PROMPTS,), 1, SPANS - 1)
    middle = jnp.where(order == PROMPTS // 2, 0, others)
    return jnp.where(order < PROMPTS // 2, SPANS - 1, middle).astype(jnp.int32)


def set_ends(array, own_key, smallest, largest):
    longest = array.shape.index(max(array.shape))
    spots = []
    for shift in (0, 1):
        where = [jax.random.randint(jax.random.fold_in(own_key, axis), (), 0, length) for axis, length in enumerate(array.shape)]
        where[longest] = (where[longest] + shift) % array.shape[longest]
        spots.append(tuple(where))
    return array.at[spots[0]].set(smallest).at[spots[1]].set(largest)


def shard_levels(stream_key, shape, cuts, least, largest):
    loudness, own = 1.0, jax.random.fold_in(stream_key, 6)
    for axis_at, blocks in cuts:
        draws = jnp.exp(jax.random.uniform(jax.random.fold_in(own, axis_at), (blocks,), jnp.float32, least / len(cuts), largest / len(cuts)))
        loudness = loudness * jnp.repeat(draws, shape[axis_at] // blocks).reshape([-1 if axis == axis_at else 1 for axis in range(len(shape))])
    return loudness


def rank_table(number_of, slope):
    loads = [(1 << 20) // math.isqrt(grade ** slope) + 1 for grade in range(1, number_of + 1)]
    scale = 1 + sum(loads) // (1 << 30)
    return np.cumsum(np.array([max(1, weight // scale) for weight in loads]))


def ranked(rng, shape, amount, skew):
    grid = rank_table(amount, skew)
    pick = jax.random.randint(jax.random.fold_in(rng, 1), shape, 0, int(grid[amount - 1]))
    standing = jnp.searchsorted(jnp.asarray(grid, jnp.int32), pick, side="right")
    return jax.random.permutation(jax.random.fold_in(rng, 2), amount)[standing].astype(jnp.int32)


def profile(count, total, bound, slope):
    weights = [(1 << 20) // math.isqrt(rank ** slope) + 1 for rank in range(2, count + 1)]
    spare, given = total - bound - (count - 1), [1] * (count - 1)
    while spare > 0:
        free = [i for i in range(count - 1) if given[i] < bound]
        mass, budget = sum([weights[i] for i in free]), spare
        for i in free:
            extra = min(bound - given[i], max(1, budget * weights[i] // mass), spare)
            given[i] = given[i] + extra
            spare = spare - extra
    return np.array([bound] + given)


def ragged(own_key, amount, total, most, slope):
    if amount == 2:
        one = jax.random.randint(own_key, (), max(1, total - most), min(most, total - 1) + 1)
        return jnp.stack([one, total - one])
    sizes = jnp.asarray(profile(amount, total, most, slope), jnp.int32)
    couples = (amount - 1) // 2
    donor, sink = sizes[1:1 + 2 * couples:2], sizes[2:2 + 2 * couples:2]
    room = jnp.minimum(donor - 1, most - sink)
    passed = jax.random.randint(jax.random.fold_in(own_key, 1), (couples,), 0, 1 << 20) % (room + 1)
    sizes = sizes.at[1:1 + 2 * couples:2].set(donor - passed).at[2:2 + 2 * couples:2].set(sink + passed)
    return sizes[jax.random.permutation(jax.random.fold_in(own_key, 2), amount)]


def normal_values(own_key, dims, deviation, most, shards=(), kind=jnp.bfloat16):
    result = jax.random.normal(own_key, dims, jnp.float32) * deviation
    if len(shards) > 0:
        result = shard_levels(own_key, dims, shards, -0.22, 0.18) * result
    return jnp.clip(result, min=-most, max=most).astype(kind)


def setup_inputs(seed: int = 0) -> dict:
    splits = jax.random.split(jax.random.key(seed), 13)
    prefill_x = normal_values(splits[0], (PROMPTS * SPAN, D), 1.0, 6.0, ((0, 8), (1, 16)))
    span_index = draw_span_index(jax.random.fold_in(splits[12], 71), 0)
    prefix_pages = jax.vmap(lambda own: jax.random.permutation(own, PRE_POOL))(jax.random.split(splits[2], PROMPTS)).reshape((PROMPTS, PRE_POOL)).astype(jnp.int32)
    prefix_cache = draw_prefix_cache(jax.random.fold_in(splits[12], 71), 0)
    decode_x = normal_values(splits[4], (2, PROMPTS * DECODE, D), 1.0, 6.0, ((1, 8), (2, 16)))
    decode_len = jax.vmap(lambda own: ragged(own, DEC_DEV, DEC_DEV * MEAN_LEN, MOST_LEN, 2))(jax.random.split(splits[5], PROMPTS * SPLIT)).reshape((PROMPTS, SPLIT, DEC_DEV)).astype(jnp.int32)
    page_order = jax.vmap(lambda own: jax.random.permutation(own, POOL_DEV))(jax.random.split(splits[6], PROMPTS * SPLIT)).reshape((PROMPTS, SPLIT, POOL_DEV)).astype(jnp.int32)
    assignment = set_ends(ranked(splits[7], (PROMPTS,), PROMPTS, 2), jax.random.fold_in(splits[7], 3), 0, PROMPTS - 1).astype(jnp.int32)
    kv_cache = draw_kv_cache(jax.random.fold_in(splits[12], 71), 0)
    w_query = normal_values(splits[9], (D, HEADS * HEAD_DIM), D ** -0.5, 0.0625, ((1, 16),))
    w_keyval = normal_values(splits[10], (D, 2 * KV_HEADS * HEAD_DIM), D ** -0.5, 0.0625, ((1, 16),))
    w_out = normal_values(splits[11], (HEADS * HEAD_DIM, D), (HEADS * HEAD_DIM) ** -0.5, 0.0625, ((0, 16),))
    return dict(prefill_x=prefill_x, span_index=span_index, prefix_pages=prefix_pages, prefix_cache=prefix_cache, decode_x=decode_x, decode_len=decode_len, page_order=page_order, assignment=assignment, kv_cache=kv_cache, w_query=w_query, w_keyval=w_keyval, w_out=w_out)


rope_base = 500000.0
masked_score = -1e30


def rotary(values, positions):
    half = values.shape[-1] // 2
    exponent = jnp.arange(half, dtype=jnp.float32) * (2.0 / values.shape[-1])
    angles = positions.astype(jnp.float32)[..., None] * (rope_base ** -exponent)
    cosine = jnp.cos(angles)
    sine = jnp.sin(angles)
    first = values[..., :half]
    second = values[..., half:]
    return jnp.concatenate([first * cosine - second * sine, second * cosine + first * sine], -1)


def softmax_rounded(scores):
    raised = jnp.exp(scores - jnp.max(scores, -1, keepdims=True))
    return (raised / jnp.sum(raised, -1, keepdims=True)).astype(jnp.bfloat16)


def product(form, left, right):
    return jnp.einsum(form, left.astype(jnp.float32), right.astype(jnp.float32), precision=lax.Precision.HIGHEST)


def head_sums(heads, w_out):
    width = (HEADS // N_TP) * HEAD_DIM
    total = jnp.zeros((heads.shape[0], w_out.shape[1]), jnp.float32)
    for device in range(N_TP):
        part = jnp.dot(heads[:, device * width:(device + 1) * width], w_out[device * width:(device + 1) * width], preferred_element_type=jnp.float32).astype(jnp.bfloat16)
        total = total + lax.optimization_barrier(part).astype(jnp.float32)
    return total.astype(jnp.bfloat16)


def reference(prefill_x, span_index, prefix_pages, prefix_cache, decode_x, decode_len, page_order, assignment, kv_cache, w_query, w_keyval, w_out):
    prompts = span_index.shape[0]
    split = N_TP // KV_HEADS
    group_size = HEADS // KV_HEADS
    dec_dev = DECODE // split
    pool_dev = page_order.shape[2]
    pre_pool = prefix_pages.shape[1]
    pre_rows = pre_pool * PAGE
    context_rows = pre_rows + SPAN
    scale = HEAD_DIM ** -0.5
    spots = span_index[:, None] * SPAN + jnp.arange(SPAN, dtype=jnp.int32)[None, :]
    query_all = jnp.dot(prefill_x, w_query, preferred_element_type=jnp.float32).reshape(prompts, SPAN, KV_HEADS, group_size, HEAD_DIM)
    queries = rotary(query_all, spots[:, :, None, None]).astype(jnp.bfloat16)
    pair_all = jnp.dot(prefill_x, w_keyval, preferred_element_type=jnp.float32).astype(jnp.bfloat16).reshape(prompts, SPAN, KV_HEADS, 2, HEAD_DIM)
    pre_keys = rotary(pair_all[:, :, :, 0].astype(jnp.float32), spots[:, :, None]).astype(jnp.bfloat16)
    pre_values = pair_all[:, :, :, 1]
    causal = jnp.arange(SPAN)[:, None] >= jnp.arange(SPAN)[None, :]
    prior_index = jnp.arange(pre_rows, dtype=jnp.int32)
    head_rows = []
    contexts = []
    for prompt in range(prompts):
        pools = prefix_cache[prompt].reshape(KV_HEADS, split, pre_pool, PAGE, 2 * HEAD_DIM)[:, 0]
        prior = pools[:, prefix_pages[prompt]].reshape(KV_HEADS, pre_rows, 2 * HEAD_DIM)
        prior_scores = product("qhed,hkd->heqk", queries[prompt], prior[..., :HEAD_DIM]) * scale
        prior_live = prior_index < span_index[prompt] * SPAN
        prior_scores = jnp.where(prior_live[None, None, None, :], prior_scores, masked_score)
        own_scores = product("qhed,khd->heqk", queries[prompt], pre_keys[prompt]) * scale
        own_scores = jnp.where(causal[None, None], own_scores, masked_score)
        weights = softmax_rounded(jnp.concatenate([prior_scores, own_scores], -1))
        heads = product("heqk,hkd->qhed", weights[..., :pre_rows], prior[..., HEAD_DIM:])
        heads = heads + product("heqk,khd->qhed", weights[..., pre_rows:], pre_values[prompt])
        head_rows.append(heads.astype(jnp.bfloat16).reshape(SPAN, HEADS * HEAD_DIM))
        fresh_rows = jnp.concatenate([pre_keys[prompt], pre_values[prompt]], -1).transpose(1, 0, 2)
        contexts.append(jnp.concatenate([prior, fresh_rows], 1))
    pre_heads = jnp.concatenate(head_rows, 0)
    prefill_out = head_sums(pre_heads, w_out)

    finished = span_index == SPANS - 1
    rows_all = decode_x.reshape(-1, D)
    dec_query = jnp.dot(rows_all, w_query, preferred_element_type=jnp.float32).reshape(2, prompts, DECODE, KV_HEADS, group_size, HEAD_DIM)
    dec_pair = jnp.dot(rows_all, w_keyval, preferred_element_type=jnp.float32).astype(jnp.bfloat16).reshape(2, prompts, DECODE, KV_HEADS, 2, HEAD_DIM)
    sources = jnp.arange(prompts, dtype=jnp.int32)
    sequence_ids = jnp.arange(DECODE, dtype=jnp.int32)
    step_order = jnp.arange(2)[:, None] >= jnp.arange(2)[None, :]
    results = []
    for group in range(prompts):
        to_here = (assignment == group) & finished
        ranks = jnp.sum(to_here[None, :] & (sources[None, :] < sources[:, None]), 1).astype(jnp.int32)
        owner = ((ranks % split) * dec_dev + ranks // split).astype(jnp.int32)
        ownership = (owner[None, :] == sequence_ids[:, None]) & to_here[None, :]
        has_context = jnp.any(ownership, 1)
        lengths = decode_len[group].reshape(DECODE)
        base = jnp.where(has_context, context_rows, lengths).astype(jnp.int32)
        positions = base[None, :] + jnp.arange(2, dtype=jnp.int32)[:, None]
        group_queries = rotary(dec_query[:, group], positions[:, :, None, None]).astype(jnp.bfloat16)
        new_keys = rotary(dec_pair[:, group, :, :, 0].astype(jnp.float32), positions[:, :, None]).astype(jnp.bfloat16)
        new_values = dec_pair[:, group, :, :, 1]
        counts = (decode_len[group] + PAGE - 1) // PAGE
        firsts = jnp.cumsum(counts, 1) - counts
        slots = jnp.clip(firsts[:, :, None] + jnp.arange(MAX_PAGES, dtype=jnp.int32)[None, None, :], 0, pool_dev - 1).astype(jnp.int32)
        page_ids = jnp.take_along_axis(page_order[group], slots.reshape(split, -1), axis=1).reshape(split, dec_dev, MAX_PAGES)
        pools = kv_cache[group].reshape(KV_HEADS, split, pool_dev, PAGE, 2 * HEAD_DIM)
        cached = jnp.stack([pools[:, part][:, page_ids[part]] for part in range(split)], 1)
        cached = cached.reshape(KV_HEADS, DECODE, MAX_PAGES * PAGE, 2 * HEAD_DIM)
        live = jnp.arange(MAX_PAGES * PAGE)[None, :] < lengths[:, None]
        pool_scores = product("tnhed,hncd->nthec", group_queries, cached[..., :HEAD_DIM]) * scale
        pool_scores = jnp.where(live[:, None, None, None, :], pool_scores, masked_score)
        fresh_scores = product("tnhed,unhd->ntheu", group_queries, new_keys) * scale
        fresh_scores = jnp.where(step_order[None, :, None, None, :], fresh_scores, masked_score)
        joined = softmax_rounded(jnp.concatenate([pool_scores, fresh_scores], -1))
        attended = product("nthec,hncd->tnhed", joined[..., :MAX_PAGES * PAGE], cached[..., HEAD_DIM:])
        attended = attended + product("ntheu,unhd->tnhed", joined[..., MAX_PAGES * PAGE:], new_values)
        attended = attended.astype(jnp.bfloat16)
        for source in range(prompts):
            slot = owner[source]
            query_row = lax.dynamic_index_in_dim(group_queries, slot, 1, keepdims=False)
            key_row = lax.dynamic_index_in_dim(new_keys, slot, 1, keepdims=False)
            value_row = lax.dynamic_index_in_dim(new_values, slot, 1, keepdims=False)
            context = contexts[source]
            context_scores = product("thed,hcd->thec", query_row, context[..., :HEAD_DIM]) * scale
            own_scores = product("thed,uhd->theu", query_row, key_row) * scale
            own_scores = jnp.where(step_order[:, None, None, :], own_scores, masked_score)
            weights = softmax_rounded(jnp.concatenate([context_scores, own_scores], -1))
            taken = product("thec,hcd->thed", weights[..., :context_rows], context[..., HEAD_DIM:])
            taken = taken + product("theu,uhd->thed", weights[..., context_rows:], value_row)
            chosen = (sequence_ids == slot) & to_here[source]
            attended = jnp.where(chosen[None, :, None, None, None], taken.astype(jnp.bfloat16)[:, None], attended)
        results.append(attended.reshape(2, DECODE, HEADS * HEAD_DIM))
    dec_heads = jnp.stack(results, 1).reshape(2 * prompts * DECODE, HEADS * HEAD_DIM)
    decode_out = head_sums(dec_heads, w_out).reshape(2, prompts * DECODE, D)
    return (prefill_out, decode_out)
```

```python
import functools

import jax
import jax.numpy as jnp
from jax import lax
from jax.experimental import pallas as pl
from jax.experimental.pallas import tpu as pltpu
from jax.sharding import PartitionSpec as P

KV_HEADS = 8
HEAD_DIM = 128
SPANS = 8
PAGE = 16
MAX_PAGES = 32
RING = 4
BLOCKS = RING * RING
MESH = pl.DeviceIdType.MESH

rope_base = 500000.0
masked_score = -1e30


def place(dz, dx):
    return (dz % RING) * RING + dx % RING


def neighbours():
    me = lax.axis_index("tp")
    z = me // RING
    x = me % RING
    return {
        ("z", 1): ((z + 1) % RING) * RING + x,
        ("z", -1): ((z + RING - 1) % RING) * RING + x,
        ("x", 1): z * RING + (x + 1) % RING,
        ("x", -1): z * RING + (x + RING - 1) % RING,
    }


def greet(near):
    barrier = pltpu.get_barrier_semaphore()
    for device in near.values():
        pl.semaphore_signal(barrier, inc=1, device_id={"tp": device}, device_id_type=MESH)
    pl.semaphore_wait(barrier, len(near))


def absolute(dz, dx):
    me = lax.axis_index("tp")
    z = me // RING
    x = me % RING
    return ((z + dz) % RING) * RING + (x + dx) % RING


def axes_of(half, first):
    return ("x", "z") if (half == 0) == first else ("z", "x")


class Copies:
    def __init__(self, near, send, receive):
        self.near, self.send, self.receive = near, send, receive
        self.made = {}

    def start(self, name, axis, step, source, target):
        index = len(self.made)
        copy = pltpu.make_async_remote_copy(
            src_ref=source,
            dst_ref=target,
            send_sem=self.send.at[index],
            recv_sem=self.receive.at[index],
            device_id={"tp": self.near[axis, step]},
            device_id_type=MESH,
        )
        copy.start()
        self.made[name] = copy

    def arrive(self, name):
        self.made[name].wait_recv()

    def sent(self):
        for copy in self.made.values():
            copy.wait_send()


class Gather:
    def __init__(self, own, held, copies):
        self.own, self.held, self.copies = own, held, copies
        self.rows = own.shape[0]

    def slot(self, half, d1, d2):
        return place(d2, d1) if half == 0 else place(d1, d2)

    def part(self, half, d1, d2, quarter=None):
        count = self.rows // 2
        first = half * count
        if quarter is not None:
            count = count // 2
            first = first + quarter * count
        slot = self.slot(half, d1, d2)
        block = self.own if slot == 0 else self.held.at[slot]
        return block.at[pl.ds(first, count)]

    def first_sends(self):
        for half in (0, 1):
            axis = axes_of(half, True)[0]
            for step in (1, -1):
                self.copies.start(
                    ("1", half, step), axis, step, self.part(half, 0, 0), self.part(half, -step, 0)
                )
        self.second_sends(0)

    def second_sends(self, d1):
        for half in (0, 1):
            self.second_send(half, d1)

    def second_send(self, half, d1):
        axis = axes_of(half, True)[1]
        for step in (1, -1):
            self.copies.start(
                ("2", half, d1, step),
                axis,
                step,
                self.part(half, d1, 0),
                self.part(half, d1, -step),
            )

    def near_arrive(self):
        for half in (0, 1):
            axis = axes_of(half, True)[0]
            for step in (1, -1):
                quarter = 0 if step == 1 else 1
                self.copies.arrive(("1", half, step))
                self.copies.start(
                    ("1f", half, step),
                    axis,
                    step,
                    self.part(half, -step, 0, quarter),
                    self.part(half, -2 * step, 0, quarter),
                )
                self.second_send(half, -step)
        return [(half, d1, 0) for half in (0, 1) for d1 in (-1, 1)]

    def far_arrive(self):
        for half in (0, 1):
            for step in (1, -1):
                self.copies.arrive(("1f", half, step))
            self.second_send(half, 2)
        return [(half, 2, 0) for half in (0, 1)]

    def line_arrive(self, d1):
        for half in (0, 1):
            axis = axes_of(half, True)[1]
            for step in (1, -1):
                quarter = 0 if step == 1 else 1
                self.copies.arrive(("2", half, d1, step))
                self.copies.start(
                    ("2f", half, d1, step),
                    axis,
                    step,
                    self.part(half, d1, -step, quarter),
                    self.part(half, d1, -2 * step, quarter),
                )
        return [(half, d1, d2) for half in (0, 1) for d2 in (-1, 1)]

    def last_arrive(self, d1):
        for half in (0, 1):
            for step in (1, -1):
                self.copies.arrive(("2f", half, d1, step))
        return [(half, d1, 2) for half in (0, 1)]


class Scatter:
    def __init__(self, terms, relays, halves, relay2, halves2, out, copies):
        self.terms, self.relays, self.halves = terms, relays, halves
        self.relay2, self.halves2, self.out, self.copies = relay2, halves2, out, copies
        self.rows = terms.shape[1]

    def part(self, half, df, ds, quarter=None):
        count = self.rows // 2
        first = half * count
        if quarter is not None:
            count = count // 2
            first = first + quarter * count
        slot = place(df, ds) if half == 0 else place(ds, df)
        return self.terms.at[slot, pl.ds(first, count)]

    def relay_send(self, ds):
        for half in (0, 1):
            axis = axes_of(half, False)[0]
            for quarter, step in ((0, 1), (1, -1)):
                self.copies.start(
                    ("1r", half, ds, step),
                    axis,
                    step,
                    self.part(half, 2, ds, quarter),
                    self.relays.at[half, ds % RING, quarter],
                )

    def near_send(self, ds):
        for half in (0, 1):
            axis = axes_of(half, False)[0]
            for quarter, step in ((0, 1), (1, -1)):
                self.copies.arrive(("1r", half, ds, step))
                own = self.part(half, step, ds, quarter)
                added = self.relays[half, ds % RING, quarter].astype(jnp.float32)
                own[...] = (own[...].astype(jnp.float32) + added).astype(jnp.bfloat16)
                self.copies.start(
                    ("1", half, ds, step),
                    axis,
                    step,
                    self.part(half, step, ds),
                    self.halves.at[half, ds % RING, quarter],
                )

    def line_sum(self, ds):
        for half in (0, 1):
            for step in (1, -1):
                self.copies.arrive(("1", half, ds, step))
            own = self.part(half, 0, ds)
            total = own[...].astype(jnp.float32)
            for side in (0, 1):
                total = total + self.halves[half, ds % RING, side].astype(jnp.float32)
            own[...] = total.astype(jnp.bfloat16)

    def relay_send2(self):
        for half in (0, 1):
            axis = axes_of(half, False)[1]
            for quarter, step in ((0, 1), (1, -1)):
                self.copies.start(
                    ("2r", half, step),
                    axis,
                    step,
                    self.part(half, 0, 2, quarter),
                    self.relay2.at[half, quarter],
                )

    def near_send2(self):
        for half in (0, 1):
            axis = axes_of(half, False)[1]
            for quarter, step in ((0, 1), (1, -1)):
                self.copies.arrive(("2r", half, step))
                own = self.part(half, 0, step, quarter)
                added = self.relay2[half, quarter].astype(jnp.float32)
                own[...] = (own[...].astype(jnp.float32) + added).astype(jnp.bfloat16)
                self.copies.start(
                    ("2", half, step),
                    axis,
                    step,
                    self.part(half, 0, step),
                    self.halves2.at[half, quarter],
                )

    def finish(self):
        count = self.rows // 2
        for half in (0, 1):
            for step in (1, -1):
                self.copies.arrive(("2", half, step))
            total = self.part(half, 0, 0)[...].astype(jnp.float32)
            for side in (0, 1):
                total = total + self.halves2[half, side].astype(jnp.float32)
            self.out[pl.ds(half * count, count)] = total.astype(jnp.bfloat16)


def project_kernel(
    pre_x, dec_x, w_query, w_keyval, pre_out, dec_out, pre_held, dec_held, weights, load, send, receive
):
    near = neighbours()
    depth, wide = pre_x.shape[1], w_query.shape[1]
    loads = []
    for slot in range(BLOCKS):
        origin = absolute(slot // RING, slot % RING)
        rows = pl.ds(pl.multiple_of(origin * depth, depth), depth)
        loads.append(
            (
                pltpu.make_async_copy(
                    w_query.at[rows], weights.at[slot, :, pl.ds(0, wide)], load.at[0, slot]
                ),
                pltpu.make_async_copy(
                    w_keyval.at[rows],
                    weights.at[slot, :, pl.ds(wide, w_keyval.shape[1])],
                    load.at[1, slot],
                ),
            )
        )
    order = [place(*d) for d in ((0, 0), (0, -1), (0, 1), (-1, 0), (1, 0), (0, 2), (2, 0))]
    order = order + [slot for slot in range(BLOCKS) if slot not in order]
    for slot in order:
        for copy in loads[slot]:
            copy.start()
    greet(near)
    loaded = set()

    def multiply(gather, total, parts):
        for half, d1, d2 in parts:
            slot = gather.slot(half, d1, d2)
            if slot not in loaded:
                loaded.add(slot)
                for copy in loads[slot]:
                    copy.wait()
            count = gather.rows // 2
            rows = pl.ds(half * count, count)
            product = jnp.dot(
                gather.part(half, d1, d2)[...], weights[slot], preferred_element_type=jnp.float32
            )
            if slot == 0:
                total[rows] = product
            else:
                total[rows] += product

    pre = Gather(pre_x, pre_held, Copies(near, send.at[0], receive.at[0]))
    dec = Gather(dec_x, dec_held, Copies(near, send.at[1], receive.at[1]))
    pre.first_sends()
    multiply(pre, pre_out, [(0, 0, 0), (1, 0, 0)])
    multiply(pre, pre_out, pre.near_arrive())
    multiply(pre, pre_out, pre.far_arrive())
    for d1 in (0, -1, 1, 2):
        parts = pre.line_arrive(d1)
        if d1 == 2:
            dec.first_sends()
        multiply(pre, pre_out, parts)
    multiply(dec, dec_out, [(0, 0, 0), (1, 0, 0)])
    for d1 in (0, -1, 1, 2):
        multiply(pre, pre_out, pre.last_arrive(d1))
    multiply(dec, dec_out, dec.near_arrive())
    multiply(dec, dec_out, dec.far_arrive())
    for d1 in (0, -1, 1, 2):
        multiply(dec, dec_out, dec.line_arrive(d1))
    for d1 in (0, -1, 1, 2):
        multiply(dec, dec_out, dec.last_arrive(d1))
    pre.copies.sent()
    dec.copies.sent()


def project(pre_x, dec_x, w_query, w_keyval):
    wide = w_query.shape[1] + w_keyval.shape[1]
    depth = pre_x.shape[1]
    vmem = pl.BlockSpec(memory_space=pltpu.VMEM)
    hbm = pl.BlockSpec(memory_space=pl.ANY)
    return pl.pallas_call(
        project_kernel,
        out_shape=(
            jax.ShapeDtypeStruct((pre_x.shape[0], wide), jnp.float32),
            jax.ShapeDtypeStruct((dec_x.shape[0], wide), jnp.float32),
        ),
        in_specs=[vmem, vmem, hbm, hbm],
        out_specs=(vmem, vmem),
        scratch_shapes=[
            pltpu.VMEM((BLOCKS,) + pre_x.shape, jnp.bfloat16),
            pltpu.VMEM((BLOCKS,) + dec_x.shape, jnp.bfloat16),
            pltpu.VMEM((BLOCKS, depth, wide), jnp.bfloat16),
            pltpu.SemaphoreType.DMA((2, BLOCKS)),
            pltpu.SemaphoreType.DMA((2, 40)),
            pltpu.SemaphoreType.DMA((2, 40)),
        ],
        compiler_params=pltpu.CompilerParams(
            collective_id=0, has_side_effects=True, vmem_limit_bytes=48 * 2**20
        ),
        name="gather_project",
    )(pre_x, dec_x, w_query, w_keyval)


ORDER = (
    ((2, 2),),
    ((2, -1), (-1, 2)),
    ((2, 1), (1, 2)),
    ((2, 0), (0, 2)),
    ((-1, -1), (-1, 1), (1, -1), (1, 1)),
    ((-1, 0), (1, 0), (0, -1), (0, 1)),
    ((0, 0),),
)


def output_kernel(
    pre_heads,
    dec_heads,
    w_out,
    pre_out,
    dec_out,
    weights,
    pre_terms,
    pre_relays,
    pre_halves,
    pre_relay2,
    pre_halves2,
    dec_terms,
    dec_relays,
    dec_halves,
    dec_relay2,
    dec_halves2,
    load,
    send,
    receive,
):
    near = neighbours()
    width = pre_out.shape[1]
    loads = {}
    for blocks in ORDER:
        for dz, dx in blocks:
            slot = place(dz, dx)
            columns = pl.ds(pl.multiple_of(absolute(dz, dx) * width, width), width)
            loads[slot] = pltpu.make_async_copy(
                w_out.at[:, columns], weights.at[slot], load.at[slot]
            )
            loads[slot].start()
    greet(near)
    loaded = set()

    def terms(heads, kept, blocks):
        for dz, dx in blocks:
            slot = place(dz, dx)
            if slot not in loaded:
                loaded.add(slot)
                loads[slot].wait()
            kept[slot] = jnp.dot(
                heads[...], weights[slot], preferred_element_type=jnp.float32
            ).astype(jnp.bfloat16)

    pre = Scatter(
        pre_terms, pre_relays, pre_halves, pre_relay2, pre_halves2, pre_out,
        Copies(near, send.at[0], receive.at[0]),
    )
    dec = Scatter(
        dec_terms, dec_relays, dec_halves, dec_relay2, dec_halves2, dec_out,
        Copies(near, send.at[1], receive.at[1]),
    )
    for scatter, heads, kept in ((pre, pre_heads, pre_terms), (dec, dec_heads, dec_terms)):
        for index, ds in enumerate((2, -1, 1, 0)):
            terms(heads, kept, ORDER[index])
            scatter.relay_send(ds)
        scatter.near_send(2)
        terms(heads, kept, ORDER[4])
        scatter.near_send(-1)
        scatter.near_send(1)
        terms(heads, kept, ORDER[5])
        scatter.near_send(0)
        terms(heads, kept, ORDER[6])
    for scatter in (pre, dec):
        scatter.line_sum(2)
        scatter.relay_send2()
        scatter.line_sum(-1)
        scatter.line_sum(1)
        scatter.near_send2()
        scatter.line_sum(0)
        scatter.finish()
    pre.copies.sent()
    dec.copies.sent()


def scatter_scratch(rows, width):
    half, quarter = rows // 2, rows // 4
    return [
        pltpu.VMEM((BLOCKS, rows, width), jnp.bfloat16),
        pltpu.VMEM((2, RING, 2, quarter, width), jnp.bfloat16),
        pltpu.VMEM((2, RING, 2, half, width), jnp.bfloat16),
        pltpu.VMEM((2, 2, quarter, width), jnp.bfloat16),
        pltpu.VMEM((2, 2, half, width), jnp.bfloat16),
    ]


def output(pre_heads, dec_heads, w_out):
    width = w_out.shape[1] // BLOCKS
    vmem = pl.BlockSpec(memory_space=pltpu.VMEM)
    hbm = pl.BlockSpec(memory_space=pl.ANY)
    return pl.pallas_call(
        output_kernel,
        out_shape=(
            jax.ShapeDtypeStruct((pre_heads.shape[0], width), jnp.bfloat16),
            jax.ShapeDtypeStruct((dec_heads.shape[0], width), jnp.bfloat16),
        ),
        in_specs=[vmem, vmem, hbm],
        out_specs=(vmem, vmem),
        scratch_shapes=[pltpu.VMEM((BLOCKS, w_out.shape[0], width), jnp.bfloat16)]
        + scatter_scratch(pre_heads.shape[0], width)
        + scatter_scratch(dec_heads.shape[0], width)
        + [
            pltpu.SemaphoreType.DMA((BLOCKS,)),
            pltpu.SemaphoreType.DMA((2, 40)),
            pltpu.SemaphoreType.DMA((2, 40)),
        ],
        compiler_params=pltpu.CompilerParams(
            collective_id=1, has_side_effects=True, vmem_limit_bytes=48 * 2**20
        ),
        name="project_scatter",
    )(pre_heads, dec_heads, w_out)


def from_partner(value, axis, distance):
    mask = 2**distance
    pairs = [(source, source ^ mask) for source in range(lax.axis_size(axis))]
    return lax.ppermute(value, axis, pairs)


def rotary(values, positions):
    half = values.shape[-1] // 2
    exponent = jnp.arange(half, dtype=jnp.float32) * (2.0 / values.shape[-1])
    angles = positions.astype(jnp.float32)[..., None] * rope_base ** (-exponent)
    cosine = jnp.cos(angles)
    sine = jnp.sin(angles)
    first = values[..., :half]
    second = values[..., half:]
    return jnp.concatenate([first * cosine - second * sine, second * cosine + first * sine], -1)


def ordered(mine, theirs, member, axis):
    return jnp.where(
        member == 0, jnp.concatenate([mine, theirs], axis), jnp.concatenate([theirs, mine], axis)
    )


def joined_softmax(first, second):
    highest = jnp.maximum(jnp.max(first, -1), jnp.max(second, -1))[..., None]
    first = jnp.exp(first - highest)
    second = jnp.exp(second - highest)
    totals = (jnp.sum(first, -1) + jnp.sum(second, -1))[..., None]
    return (first / totals).astype(jnp.bfloat16), (second / totals).astype(jnp.bfloat16)


def einsum(form, left, right):
    return jnp.einsum(form, left, right, preferred_element_type=jnp.float32)


def body(
    prefill_x,
    span_index,
    prefix_pages,
    prefix_cache,
    decode_x,
    decode_len,
    page_order,
    assignment,
    kv_cache,
    w_query,
    w_keyval,
    w_out,
):
    split = lax.axis_size("tp") // KV_HEADS
    member = lax.axis_index("tp") % split
    group = lax.axis_index("grp")
    prompts = lax.axis_size("grp")
    span = prefill_x.shape[0]
    decode = decode_x.shape[1]
    rows = 2 * decode
    dec_dev = decode // split
    query_wide = w_query.shape[1]
    heads_dev = query_wide // HEAD_DIM
    pre_rows = prefix_cache.shape[2]
    context_rows = pre_rows + span
    scale = HEAD_DIM ** (-0.5)

    pre_all, dec_all = project(
        prefill_x, decode_x.reshape(rows, decode_x.shape[2]), w_query, w_keyval
    )
    pre_query, pre_half = pre_all[:, :query_wide], pre_all[:, query_wide:].astype(jnp.bfloat16)
    dec_query, dec_half = dec_all[:, :query_wide], dec_all[:, query_wide:].astype(jnp.bfloat16)
    halves = jnp.concatenate([pre_half, dec_half], 0)
    whole = ordered(halves, from_partner(halves, "tp", 0), member, 1)
    pre_whole, dec_whole = whole[:span], whole[span:]

    start_row = span_index[group] * span
    pre_spots = start_row + jnp.arange(span, dtype=jnp.int32)
    queries = rotary(pre_query.reshape(span, heads_dev, HEAD_DIM), pre_spots[:, None]).astype(
        jnp.bfloat16
    )
    pre_keys = rotary(pre_whole[:, :HEAD_DIM].astype(jnp.float32), pre_spots).astype(jnp.bfloat16)
    pre_values = pre_whole[:, HEAD_DIM:]
    prior = prefix_cache.reshape(pre_rows, 2 * HEAD_DIM)
    pages = pre_rows // PAGE
    page_live = jnp.any(
        (prefix_pages[0][:, None] == jnp.arange(pages, dtype=jnp.int32)[None, :])
        & (jnp.arange(pages, dtype=jnp.int32)[:, None] < start_row // PAGE),
        0,
    )
    prior_live = jnp.repeat(page_live, PAGE)
    prior_scores = einsum("qhd,kd->hqk", queries, prior[:, :HEAD_DIM]) * scale
    prior_scores = jnp.where(prior_live[None, None, :], prior_scores, masked_score)
    own_scores = einsum("qhd,kd->hqk", queries, pre_keys) * scale
    causal = jnp.arange(span)[:, None] >= jnp.arange(span)[None, :]
    own_scores = jnp.where(causal[None], own_scores, masked_score)
    prior_weights, own_weights = joined_softmax(prior_scores, own_scores)
    pre_heads = einsum("hqk,kd->qhd", prior_weights, prior[:, HEAD_DIM:])
    pre_heads = pre_heads + einsum("hqk,kd->qhd", own_weights, pre_values)
    pre_heads = pre_heads.astype(jnp.bfloat16).reshape(span, heads_dev * HEAD_DIM)

    finished = span_index == SPANS - 1
    sources = jnp.arange(prompts, dtype=jnp.int32)
    to_here = (assignment == group) & finished
    ranks = jnp.sum(to_here[None, :] & (sources[None, :] < sources[:, None]), 1)
    owner = ranks % split * dec_dev + ranks // split
    all_lengths = decode_len.reshape(decode)
    sequence_ids = jnp.arange(decode, dtype=jnp.int32)
    owned = (owner[:, None] == sequence_ids[None, :]) & to_here[:, None]
    has_context = jnp.any(owned, 0)
    base = jnp.where(has_context, context_rows, all_lengths)
    spots = base[None, :] + jnp.arange(2, dtype=jnp.int32)[:, None]
    dec_queries = rotary(
        dec_query.reshape(2, decode, heads_dev, HEAD_DIM), spots[:, :, None]
    ).astype(jnp.bfloat16)
    new_keys = rotary(
        dec_whole[:, :HEAD_DIM].astype(jnp.float32).reshape(2, decode, HEAD_DIM), spots
    ).astype(jnp.bfloat16)
    new_values = dec_whole[:, HEAD_DIM:].reshape(2, decode, HEAD_DIM)
    step_order = jnp.arange(2)[:, None] >= jnp.arange(2)[None, :]

    picks = owned.astype(jnp.bfloat16)
    steps = jnp.concatenate(
        [dec_queries.reshape(2, decode, query_wide), new_keys, new_values], -1
    )
    visiting = einsum("sj,tjc->stc", picks, steps).astype(jnp.bfloat16)
    visiting = lax.all_to_all(visiting, "grp", split_axis=0, concat_axis=0, tiled=True)
    visiting = jnp.sum(visiting.astype(jnp.float32), 0).astype(jnp.bfloat16)
    visit_queries = visiting[:, :query_wide].reshape(2, heads_dev, HEAD_DIM)
    visit_keys = visiting[:, query_wide : query_wide + HEAD_DIM]
    visit_values = visiting[:, query_wide + HEAD_DIM :]
    context = jnp.concatenate([prior, jnp.concatenate([pre_keys, pre_values], 1)], 0)
    context_scores = einsum("tgd,cd->tgc", visit_queries, context[:, :HEAD_DIM]) * scale
    step_scores = einsum("tgd,ud->tgu", visit_queries, visit_keys) * scale
    step_scores = jnp.where(step_order[:, None, :], step_scores, masked_score)
    context_weights, step_weights = joined_softmax(context_scores, step_scores)
    taken = einsum("tgc,cd->tgd", context_weights, context[:, HEAD_DIM:])
    taken = taken + einsum("tgu,ud->tgd", step_weights, visit_values)
    taken = lax.all_gather(taken.astype(jnp.bfloat16), "grp")

    block_queries = dec_queries.reshape(2, split, dec_dev, heads_dev, HEAD_DIM)
    mine = lax.dynamic_index_in_dim(block_queries, member, 1, keepdims=False)
    others = lax.dynamic_index_in_dim(block_queries, 1 - member, 1, keepdims=False)
    group_queries = ordered(mine, from_partner(others, "tp", 0), member, 2)
    my_keys = lax.dynamic_index_in_dim(
        new_keys.reshape(2, split, dec_dev, HEAD_DIM), member, 1, keepdims=False
    )
    my_values = lax.dynamic_index_in_dim(
        new_values.reshape(2, split, dec_dev, HEAD_DIM), member, 1, keepdims=False
    )
    my_lengths = lax.dynamic_index_in_dim(decode_len[0], member, 0, keepdims=False)
    my_order = lax.dynamic_index_in_dim(page_order[0], member, 0, keepdims=False)
    pool_dev = my_order.shape[0]
    counts = (my_lengths + PAGE - 1) // PAGE
    firsts = jnp.cumsum(counts) - counts
    slots = jnp.clip(
        firsts[:, None] + jnp.arange(MAX_PAGES, dtype=jnp.int32)[None, :], 0, pool_dev - 1
    )
    page_ids = my_order[slots]
    pool = kv_cache.reshape(pool_dev, PAGE, 2 * HEAD_DIM)
    cached = pool[page_ids].reshape(dec_dev, MAX_PAGES * PAGE, 2 * HEAD_DIM)
    live = jnp.arange(MAX_PAGES * PAGE)[None, :] < my_lengths[:, None]
    pool_scores = einsum("tjgd,jcd->jtgc", group_queries, cached[..., :HEAD_DIM]) * scale
    pool_scores = jnp.where(live[:, None, None, :], pool_scores, masked_score)
    fresh_scores = einsum("tjgd,ujd->jtgu", group_queries, my_keys) * scale
    fresh_scores = jnp.where(step_order[None, :, None, :], fresh_scores, masked_score)
    pool_weights, fresh_weights = joined_softmax(pool_scores, fresh_scores)
    attended = einsum("jtgc,jcd->tjgd", pool_weights, cached[..., HEAD_DIM:])
    attended = attended + einsum("jtgu,ujd->tjgd", fresh_weights, my_values)
    attended = attended.astype(jnp.bfloat16)
    keep_heads = lax.dynamic_slice_in_dim(attended, member * heads_dev, heads_dev, 2)
    away_heads = lax.dynamic_slice_in_dim(attended, (1 - member) * heads_dev, heads_dev, 2)
    own_heads = ordered(keep_heads, from_partner(away_heads, "tp", 0), member, 1)
    placed = einsum("sj,stgd->tjgd", picks, taken).astype(jnp.bfloat16)
    own_heads = jnp.where(has_context[None, :, None, None], placed, own_heads)

    prefill_out, decode_out = output(pre_heads, own_heads.reshape(rows, query_wide), w_out)
    return (prefill_out, decode_out.reshape(2, decode, -1))


def solution(mesh):
    placed = (
        P("grp", "tp"),
        P(),
        P("grp", None),
        P("grp", "tp", None, None),
        P(None, "grp", "tp"),
        P("grp", None, None),
        P("grp", None, None),
        P(),
        P("grp", "tp", None, None),
        P(None, "tp"),
        P(None, "tp"),
        P("tp", None),
    )
    return jax.shard_map(
        body,
        mesh=mesh,
        in_specs=placed,
        out_specs=(P("grp", "tp"), P(None, "grp", "tp")),
        check_vma=False,
    )
```

```python
import functools
import types

import jax
import jax.numpy as jnp
import numpy as np
from jax import lax
from jax.experimental import pallas as pl
from jax.experimental.pallas import tpu as pltpu
from jax.sharding import PartitionSpec as P

KV_HEADS = 8
HEAD_DIM = 128
SPANS = 8
PAGE = 16
MAX_PAGES = 32
RING = 4
BLOCKS = RING * RING
SPLIT = 2
GROUPS = 8
STEP_ROWS = 16
MESH = pl.DeviceIdType.MESH

rope_base = 500000.0
masked_score = -1e30


def place(dz, dx):
    return (dz % RING) * RING + dx % RING


def neighbours():
    me = lax.axis_index("tp")
    z = me // RING
    x = me % RING
    return {
        ("z", 1): ((z + 1) % RING) * RING + x,
        ("z", -1): ((z + RING - 1) % RING) * RING + x,
        ("x", 1): z * RING + (x + 1) % RING,
        ("x", -1): z * RING + (x + RING - 1) % RING,
    }


def absolute(dz, dx):
    me = lax.axis_index("tp")
    z = me // RING
    x = me % RING
    return ((z + dz) % RING) * RING + (x + dx) % RING


def axes_of(half, first):
    return ("x", "z") if (half == 0) == first else ("z", "x")


def await_bytes(region, semaphore):
    pltpu.make_async_copy(region, region, semaphore).wait()


class Copies:
    def __init__(self, near, send, receive):
        self.near, self.send, self.receive = near, send, receive
        self.index = {}

    def start(self, name, axis, step, source, target):
        index = self.index.setdefault(name, len(self.index))
        pltpu.make_async_remote_copy(
            src_ref=source,
            dst_ref=target,
            send_sem=self.send,
            recv_sem=self.receive.at[index],
            device_id={"tp": self.near[axis, step]},
            device_id_type=MESH,
        ).start()

    def arrive(self, name, region):
        await_bytes(region, self.receive.at[self.index[name]])

    def sent(self, region):
        await_bytes(region, self.send)


class Gather:
    def __init__(self, own, held, copies):
        self.own, self.held, self.copies = own, held, copies
        self.rows = own.shape[0]

    def slot(self, half, d1, d2):
        return place(d2, d1) if half == 0 else place(d1, d2)

    def part(self, half, d1, d2, quarter=None):
        count = self.rows // 2
        first = half * count
        if quarter is not None:
            count = count // 2
            first = first + quarter * count
        return self.held.at[self.slot(half, d1, d2), pl.ds(first, count)]

    def mine(self, half):
        count = self.rows // 2
        return self.held.at[0, pl.ds(half * count, count)]

    def first_sends(self):
        for half in (0, 1):
            axis = axes_of(half, True)[0]
            for step in (1, -1):
                self.copies.start(
                    ("1", half, step), axis, step, self.mine(half), self.part(half, -step, 0)
                )
        self.second_sends(0)

    def second_sends(self, d1):
        for half in (0, 1):
            self.second_send(half, d1)

    def second_send(self, half, d1):
        axis = axes_of(half, True)[1]
        for step in (1, -1):
            self.copies.start(
                ("2", half, d1, step),
                axis,
                step,
                self.part(half, d1, 0) if d1 != 0 else self.mine(half),
                self.part(half, d1, -step),
            )

    def near_arrive(self):
        for half in (0, 1):
            axis = axes_of(half, True)[0]
            for step in (1, -1):
                quarter = 0 if step == 1 else 1
                self.copies.arrive(("1", half, step), self.part(half, -step, 0))
                self.copies.start(
                    ("1f", half),
                    axis,
                    step,
                    self.part(half, -step, 0, quarter),
                    self.part(half, -2 * step, 0, quarter),
                )
                self.second_send(half, -step)
        return [(half, d1, 0) for half in (0, 1) for d1 in (-1, 1)]

    def far_arrive(self):
        for half in (0, 1):
            self.copies.arrive(("1f", half), self.part(half, 2, 0))
            self.second_send(half, 2)
        return [(half, 2, 0) for half in (0, 1)]

    def line_arrive(self, d1):
        for half in (0, 1):
            axis = axes_of(half, True)[1]
            for step in (1, -1):
                quarter = 0 if step == 1 else 1
                self.copies.arrive(("2", half, d1, step), self.part(half, d1, -step))
                self.copies.start(
                    ("2f", half, d1),
                    axis,
                    step,
                    self.part(half, d1, -step, quarter),
                    self.part(half, d1, -2 * step, quarter),
                )
        return [(half, d1, d2) for half in (0, 1) for d2 in (-1, 1)]

    def last_arrive(self, d1):
        for half in (0, 1):
            self.copies.arrive(("2f", half, d1), self.part(half, d1, 2))
        return [(half, d1, 2) for half in (0, 1)]


class Scatter:
    def __init__(self, terms, relays, halves, relay2, halves2, out, copies):
        self.terms, self.relays, self.halves = terms, relays, halves
        self.relay2, self.halves2, self.out, self.copies = relay2, halves2, out, copies
        self.rows = terms.shape[1]

    def part(self, half, df, ds, quarter=None):
        count = self.rows // 2
        first = half * count
        if quarter is not None:
            count = count // 2
            first = first + quarter * count
        slot = place(df, ds) if half == 0 else place(ds, df)
        return self.terms.at[slot, pl.ds(first, count)]

    def relay_send(self, ds):
        for half in (0, 1):
            axis = axes_of(half, False)[0]
            for quarter, step in ((0, 1), (1, -1)):
                self.copies.start(
                    ("1r", half, ds),
                    axis,
                    step,
                    self.part(half, 2, ds, quarter),
                    self.relays.at[half, ds % RING, quarter],
                )

    def near_send(self, ds):
        for half in (0, 1):
            axis = axes_of(half, False)[0]
            self.copies.arrive(("1r", half, ds), self.relays.at[half, ds % RING])
            for quarter, step in ((0, 1), (1, -1)):
                own = self.part(half, step, ds, quarter)
                added = self.relays[half, ds % RING, quarter].astype(jnp.float32)
                own[...] = (own[...].astype(jnp.float32) + added).astype(jnp.bfloat16)
                self.copies.start(
                    ("1", half, ds),
                    axis,
                    step,
                    self.part(half, step, ds),
                    self.halves.at[half, ds % RING, quarter],
                )

    def line_sum(self, ds):
        for half in (0, 1):
            self.copies.arrive(("1", half, ds), self.halves.at[half, ds % RING])
            own = self.part(half, 0, ds)
            total = own[...].astype(jnp.float32)
            for side in (0, 1):
                total = total + self.halves[half, ds % RING, side].astype(jnp.float32)
            own[...] = total.astype(jnp.bfloat16)

    def relay_send2(self):
        for half in (0, 1):
            axis = axes_of(half, False)[1]
            for quarter, step in ((0, 1), (1, -1)):
                self.copies.start(
                    ("2r", half),
                    axis,
                    step,
                    self.part(half, 0, 2, quarter),
                    self.relay2.at[half, quarter],
                )

    def near_send2(self):
        for half in (0, 1):
            axis = axes_of(half, False)[1]
            self.copies.arrive(("2r", half), self.relay2.at[half])
            for quarter, step in ((0, 1), (1, -1)):
                own = self.part(half, 0, step, quarter)
                added = self.relay2[half, quarter].astype(jnp.float32)
                own[...] = (own[...].astype(jnp.float32) + added).astype(jnp.bfloat16)
                self.copies.start(
                    ("2", half),
                    axis,
                    step,
                    self.part(half, 0, step),
                    self.halves2.at[half, quarter],
                )

    def finish(self):
        count = self.rows // 2
        for half in (0, 1):
            self.copies.arrive(("2", half), self.halves2.at[half])
            total = self.part(half, 0, 0)[...].astype(jnp.float32)
            for side in (0, 1):
                total = total + self.halves2[half, side].astype(jnp.float32)
            self.out[pl.ds(half * count, count)] = total.astype(jnp.bfloat16)


def partner():
    me = lax.axis_index("tp")
    return me + 1 - 2 * (me % SPLIT)


def greet_all(near):
    barrier = pltpu.get_barrier_semaphore()
    group = lax.axis_index("grp")
    for device in near.values():
        pl.semaphore_signal(barrier, inc=1, device_id={"tp": device}, device_id_type=MESH)
    for step in range(1, GROUPS):
        other = (group + step) % GROUPS
        pl.semaphore_signal(barrier, inc=1, device_id={"grp": other}, device_id_type=MESH)
    pl.semaphore_wait(barrier, len(near) + GROUPS - 1)


ORDER = (
    ((2, 2),),
    ((2, -1), (-1, 2)),
    ((2, 1), (1, 2)),
    ((2, 0), (0, 2)),
    ((-1, -1), (-1, 1), (1, -1), (1, 1)),
    ((-1, 0), (1, 0), (0, -1), (0, 1)),
    ((0, 0),),
)


def lane_turn(values):
    half = HEAD_DIM // 2
    return jnp.concatenate([values[:, half:], values[:, :half]], 1)


def turn_tables(positions, frequency):
    angles = positions * frequency
    lanes = lax.broadcasted_iota(jnp.int32, angles.shape, 1)
    sine = jnp.sin(angles)
    return jnp.cos(angles), jnp.where(lanes < HEAD_DIM // 2, -sine, sine)


def turn(values, cosine, sine):
    return (values * cosine + lane_turn(values) * sine).astype(jnp.bfloat16)


def dot_rows(left, right):
    return lax.dot_general(
        left, right, (((1,), (1,)), ((), ())), preferred_element_type=jnp.float32
    )


def dot(left, right):
    return jnp.dot(left, right, preferred_element_type=jnp.float32)


def layer_kernel(names, *refs):
    r = types.SimpleNamespace(**dict(zip(names, refs)))
    near = neighbours()
    me = lax.axis_index("tp")
    group = lax.axis_index("grp")
    member = me % SPLIT
    pre_x, dec_x = r.pre_x, r.dec_x
    span, depth = pre_x.shape
    rows = dec_x.shape[0]
    decode = rows // 2
    dec_dev = decode // SPLIT
    wide = r.w_query.shape[1]
    heads_dev = wide // HEAD_DIM
    pre_rows = r.prior_hbm.shape[0]
    pool_pages = r.pool_hbm.shape[0]
    scale = HEAD_DIM ** (-0.5)

    loads, out_loads = {}, {}
    order = ((0, 0), (0, -1), (0, 1), (-1, 0), (1, 0), (0, 2), (2, 0), (-1, -1), (-1, 1), (1, -1))
    order += ((1, 1), (2, -1), (2, 1), (-1, 2), (1, 2), (2, 2))
    order = [place(*offset) for offset in order]
    weights, out_weights = r.weights, r.out_weights
    for slot in order:
        origin = absolute(slot // RING, slot % RING)
        span_rows = pl.ds(pl.multiple_of(origin * depth, depth), depth)
        loads[slot] = (
            pltpu.make_async_copy(
                r.w_query.at[span_rows],
                weights.at[slot, :, pl.ds(0, wide)],
                r.load.at[slot],
            ),
            pltpu.make_async_copy(
                r.w_keyval.at[span_rows],
                weights.at[slot, :, pl.ds(wide, HEAD_DIM)],
                r.load.at[slot],
            ),
        )
    for slot in order:
        origin = absolute(slot // RING, slot % RING)
        columns = pl.ds(pl.multiple_of(origin * depth, depth), depth)
        out_loads[slot] = pltpu.make_async_copy(
            r.w_out.at[:, columns], out_weights.at[slot], r.out_load.at[slot]
        )
    prior_load = pltpu.make_async_copy(r.prior_hbm, r.prior, r.other_load.at[0])
    pre_load = pltpu.make_async_copy(pre_x, r.pre_held.at[0], r.other_load.at[1])
    dec_load = pltpu.make_async_copy(dec_x, r.dec_held.at[0], r.other_load.at[2])
    pool_loads = []
    for part in range(4):
        pages = pl.ds(part * pool_pages // 4, pool_pages // 4)
        pool_loads.append(
            pltpu.make_async_copy(r.pool_hbm.at[pages], r.pool.at[pages], r.other_load.at[3])
        )
    small_loads = [
        pltpu.make_async_copy(source, target, r.other_load.at[4 + index])
        for index, (source, target) in enumerate(
            (
                (r.span_index_hbm, r.span_index),
                (r.assignment_hbm, r.assignment),
                (r.frequency_hbm, r.frequency),
                (r.prefix_pages_hbm, r.prefix_pages),
                (r.decode_len_hbm, r.decode_len),
                (r.page_order_hbm, r.page_order),
            )
        )
    ]
    pre_load.start()
    dec_load.start()
    for copy in small_loads:
        copy.start()
    for slot in order[:5]:
        for copy in loads[slot]:
            copy.start()
    waiting = [copy for slot in order[5:] for copy in loads[slot]]
    waiting += pool_loads + [prior_load] + [out_loads[place(*d)] for d in sum(ORDER, ())]

    def load_more(count):
        for copy in waiting[:count]:
            copy.start()
        del waiting[:count]

    greet_all(near)
    loaded = set()

    def multiply(gather, total, parts):
        for half, d1, d2 in parts:
            slot = gather.slot(half, d1, d2)
            if slot not in loaded:
                loaded.add(slot)
                await_bytes(weights.at[slot], r.load.at[slot])
            count = gather.rows // 2
            at = pl.ds(half * count, count)
            product = dot(gather.part(half, d1, d2)[...], weights[slot])
            if slot == 0:
                total[at] = product
            else:
                total[at] += product

    pre = Gather(pre_x, r.pre_held, Copies(near, r.send.at[0], r.gather_receive.at[0]))
    dec = Gather(dec_x, r.dec_held, Copies(near, r.send.at[1], r.gather_receive.at[1]))
    pre_total, dec_total = r.pre_total, r.dec_total
    pre_load.wait()
    pre.first_sends()
    load_more(4)
    multiply(pre, pre_total, [(0, 0, 0), (1, 0, 0)])

    for copy in small_loads:
        copy.wait()

    span_of = [r.span_index[s] for s in range(GROUPS)]
    goes_to = [r.assignment[s] for s in range(GROUPS)]
    to_here, owner = [], []
    rank = 0 * group
    for s in range(GROUPS):
        here = jnp.where((span_of[s] == SPANS - 1) & (goes_to[s] == group), 1, 0)
        to_here.append(here)
        owner.append((rank & 1) * dec_dev + (rank >> 1))
        rank = rank + here
    start_row = r.span_index[group] * span
    frequency = r.frequency[...]

    def prior_mask():
        live_pages = start_row // PAGE
        column_page = lax.broadcasted_iota(jnp.int32, (1, pre_rows), 1) // PAGE

        def mark(index, live):
            page = r.prefix_pages[0, index]
            page = jnp.where(index < live_pages, page, -1)
            return jnp.where(column_page == page, 0.0, live)

        live = jnp.full((1, pre_rows), masked_score, jnp.float32)
        r.prior_bias[...] = lax.fori_loop(0, pre_rows // PAGE, mark, live, unroll=8)

    def pre_tables():
        spots = (start_row + lax.broadcasted_iota(jnp.int32, (span, HEAD_DIM), 0)).astype(
            jnp.float32
        )
        cosine, sine = turn_tables(spots, frequency)
        r.pre_cos[...] = cosine
        r.pre_sin[...] = sine

    def dec_tables():
        row = lax.broadcasted_iota(jnp.int32, (rows, HEAD_DIM), 0)
        sequence = row % decode

        def spread(index, base):
            length = r.decode_len[0, index // dec_dev, index % dec_dev]
            return jnp.where(sequence == index, length, base)

        base = lax.fori_loop(0, decode, spread, jnp.zeros_like(row), unroll=4)
        taken = jnp.zeros(row.shape, jnp.float32)
        for s in range(GROUPS):
            mine = jnp.where(to_here[s] == 1, owner[s], -1)
            taken = jnp.where(sequence == mine, 1.0, taken)
        base = jnp.where(taken > 0.5, pre_rows + span, base)
        cosine, sine = turn_tables((base + row // decode).astype(jnp.float32), frequency)
        r.dec_cos[...] = cosine
        r.dec_sin[...] = sine
        r.taken[...] = taken
        row = lax.broadcasted_iota(jnp.int32, (STEP_ROWS, rows), 0)
        column = lax.broadcasted_iota(jnp.int32, (STEP_ROWS, rows), 1)
        for s in range(GROUPS):
            mine = jnp.where(to_here[s] == 1, owner[s], -rows)
            picked = (column == row * decode + mine) & (row < 2)
            r.picks[pl.ds(s * STEP_ROWS, STEP_ROWS)] = jnp.where(picked, 1.0, 0.0).astype(
                jnp.bfloat16
            )

    pieces = 8
    chunk = pool_pages // pieces

    def reorder(piece):
        def move(index, carry):
            page = r.page_order[0, member, index]
            r.pages[index] = r.pool[page]
            return carry

        lax.fori_loop(piece * chunk, (piece + 1) * chunk, move, 0, unroll=4)

    pre_tables()
    load_more(6)
    multiply(pre, pre_total, pre.near_arrive())
    prior_mask()
    load_more(6)
    multiply(pre, pre_total, pre.far_arrive())
    dec_tables()
    for d1 in (0, -1, 1, 2):
        parts = pre.line_arrive(d1)
        load_more(4)
        if d1 == 2:
            dec_load.wait()
            dec.first_sends()
        multiply(pre, pre_total, parts)
    multiply(dec, dec_total, [(0, 0, 0), (1, 0, 0)])
    await_bytes(r.pool, r.other_load.at[3])
    r.pages[pl.ds(pool_pages, MAX_PAGES)] = jnp.zeros(
        (MAX_PAGES, PAGE, 2 * HEAD_DIM), jnp.bfloat16
    )
    for index, d1 in enumerate((0, -1, 1, 2)):
        multiply(pre, pre_total, pre.last_arrive(d1))
        load_more(3)
        reorder(2 * index)
        reorder(2 * index + 1)
    load_more(len(waiting))

    def swap(kind, source, target, device):
        pltpu.make_async_remote_copy(
            src_ref=source,
            dst_ref=target,
            send_sem=r.small_send.at[kind],
            recv_sem=r.small_receive.at[kind],
            device_id=device,
            device_id_type=MESH,
        ).start()

    def swapped(kind, region):
        await_bytes(region, r.small_receive.at[kind])

    pre_swap, dec_swap, query_swap, visit_swap, take_swap, back_swap = range(6)
    others = pl.ds(1, GROUPS - 1)
    beside = {"tp": partner()}
    pre_pair, dec_pair = r.pre_pair, r.dec_pair
    pre_pair[member] = pre_total[:, wide:].astype(jnp.bfloat16)
    swap(pre_swap, pre_pair.at[member], pre_pair.at[member], beside)
    cosine, sine = r.pre_cos[...], r.pre_sin[...]
    for head in range(heads_dev):
        at = pl.ds(head * HEAD_DIM, HEAD_DIM)
        r.pre_query[:, at] = turn(pre_total[:, at], cosine, sine)
    dec_parts = dec.near_arrive()
    multiply(dec, dec_total, dec_parts)
    swapped(pre_swap, pre_pair.at[1 - member])
    r.pre_key[...] = turn(
        pre_pair[0].astype(jnp.float32), r.pre_cos[...], r.pre_sin[...]
    )
    prior_load.wait()
    prior_bias = r.prior_bias
    prior = r.prior
    block = span // 2

    def attend(head, part):
        at = pl.ds(head * HEAD_DIM, HEAD_DIM)
        here = pl.ds(part * block, block)
        query = r.pre_query[here, at]
        prior_scores = dot_rows(query, prior[:, pl.ds(0, HEAD_DIM)]) * scale + prior_bias[...]
        own_scores = dot_rows(query, r.pre_key[...]) * scale
        row = lax.broadcasted_iota(jnp.int32, own_scores.shape, 0) + part * block
        column = lax.broadcasted_iota(jnp.int32, own_scores.shape, 1)
        own_scores = jnp.where(row >= column, own_scores, masked_score)
        highest = jnp.maximum(
            jnp.max(prior_scores, 1, keepdims=True), jnp.max(own_scores, 1, keepdims=True)
        )
        prior_raised = jnp.exp(prior_scores - highest)
        own_raised = jnp.exp(own_scores - highest)
        total = jnp.sum(prior_raised, 1, keepdims=True) + jnp.sum(own_raised, 1, keepdims=True)
        values = dot(prior_raised.astype(jnp.bfloat16), prior[:, pl.ds(HEAD_DIM, HEAD_DIM)])
        values = values + dot(own_raised.astype(jnp.bfloat16), pre_pair[1])
        r.pre_heads[here, at] = (values / total).astype(jnp.bfloat16)

    def terms(heads, kept, blocks):
        for dz, dx in blocks:
            slot = place(dz, dx)
            if slot not in term_loaded:
                term_loaded.add(slot)
                out_loads[slot].wait()
            kept[slot] = dot(heads[...], out_weights[slot]).astype(jnp.bfloat16)

    term_loaded = set()
    pre_scatter = Scatter(
        r.pre_terms,
        r.pre_relays,
        r.pre_halves,
        r.pre_relay2,
        r.pre_halves2,
        r.pre_result,
        Copies(near, r.send.at[2], r.scatter_receive.at[0]),
    )
    dec_scatter = Scatter(
        r.dec_terms,
        r.dec_relays,
        r.dec_halves,
        r.dec_relay2,
        r.dec_halves2,
        r.dec_result,
        Copies(near, r.send.at[3], r.scatter_receive.at[1]),
    )
    pre_heads, pre_terms = r.pre_heads, r.pre_terms
    work = [(head, part) for head in range(heads_dev) for part in (0, 1)]
    events = [dec.far_arrive]
    events += [functools.partial(dec.line_arrive, d1) for d1 in (0, -1, 1, 2)]
    for index, item in enumerate(work):
        if index < len(events):
            multiply(dec, dec_total, events[index]())
        attend(*item)
    terms(pre_heads, pre_terms, sum(ORDER, ()))
    for d1 in (0, -1, 1, 2):
        if d1 == 1:
            pre_scatter.relay_send(2)
            pre_scatter.relay_send(-1)
        multiply(dec, dec_total, dec.last_arrive(d1))

    dec_pair[member] = dec_total[:, wide:].astype(jnp.bfloat16)
    swap(dec_swap, dec_pair.at[member], dec_pair.at[member], beside)
    cosine, sine = r.dec_cos[...], r.dec_sin[...]
    for head in range(heads_dev):
        at = pl.ds(head * HEAD_DIM, HEAD_DIM)
        r.steps[:, at] = turn(dec_total[:, at], cosine, sine)

    def of_member(t, which):
        return pl.ds(pl.multiple_of(t * decode + which * dec_dev, dec_dev), dec_dev)

    for t in (0, 1):
        swap(
            query_swap,
            r.steps.at[of_member(t, 1 - member), pl.ds(0, wide)],
            r.seq_query.at[member, t],
            beside,
        )
        r.seq_query[member, t] = r.steps[of_member(t, member), pl.ds(0, wide)]

    pre_scatter.relay_send(1)
    pre_scatter.relay_send(0)
    pre_scatter.near_send(2)

    swapped(dec_swap, dec_pair.at[1 - member])
    r.steps[:, pl.ds(wide, HEAD_DIM)] = turn(
        dec_pair[0].astype(jnp.float32), r.dec_cos[...], r.dec_sin[...]
    )
    r.steps[:, pl.ds(wide + HEAD_DIM, HEAD_DIM)] = dec_pair[1]
    r.visit_out[...] = dot(r.picks[...], r.steps[...]).astype(jnp.bfloat16)
    for step in range(1, GROUPS):
        other = (group + step) % GROUPS
        here = pl.ds(pl.multiple_of(other * STEP_ROWS, STEP_ROWS), STEP_ROWS)
        swap(visit_swap, r.visit_out.at[here], r.visit_in.at[step], {"grp": other})
    for t in (0, 1):
        here = pl.ds(t * dec_dev, dec_dev)
        r.seq_key[here] = r.steps[of_member(t, member), pl.ds(wide, HEAD_DIM)].astype(
            jnp.float32
        )
        r.seq_value[here] = r.steps[
            of_member(t, member), pl.ds(wide + HEAD_DIM, HEAD_DIM)
        ].astype(jnp.float32)
    pre_scatter.near_send(-1)
    swapped(query_swap, r.seq_query.at[1 - member])
    for head in range(heads_dev):
        lines = r.seq_query[:, :, :, pl.ds(head * HEAD_DIM, HEAD_DIM)]
        r.seq_rows[pl.ds(head * rows, rows)] = lines.reshape(rows, HEAD_DIM).astype(jnp.float32)

    counts = [
        (r.decode_len[0, member, index] + (PAGE - 1)) >> 4 for index in range(dec_dev)
    ]
    firsts, total_pages = [], 0
    for index in range(dec_dev):
        firsts.append(total_pages)
        total_pages = total_pages + counts[index]

    def cached_some(part):
        sequences = range(part * dec_dev // 8, (part + 1) * dec_dev // 8)
        lines = [pl.ds(index, 2 * SPLIT * heads_dev, stride=dec_dev) for index in sequences]
        pages = [pl.ds(firsts[index], MAX_PAGES) for index in sequences]
        found = []
        for at, index, here in zip(lines, sequences, pages):
            query = r.seq_rows[at, :]
            keys = r.pages[here, :, pl.ds(0, HEAD_DIM)].reshape(MAX_PAGES * PAGE, HEAD_DIM)
            scores = dot_rows(query.astype(jnp.bfloat16), keys) * scale
            column = lax.broadcasted_iota(jnp.int32, scores.shape, 1)
            scores = jnp.where(column < r.decode_len[0, member, index], scores, masked_score)
            step0 = jnp.sum(query * r.seq_key[pl.ds(index, 1)], 1, keepdims=True) * scale
            step1 = jnp.sum(query * r.seq_key[pl.ds(dec_dev + index, 1)], 1, keepdims=True) * scale
            found.append((scores, step0, step1))
        raised = []
        for scores, step0, step1 in found:
            second = lax.broadcasted_iota(jnp.int32, step1.shape, 0) % 2 == 1
            step1 = jnp.where(second, step1, masked_score)
            highest = jnp.maximum(jnp.max(scores, 1, keepdims=True), jnp.maximum(step0, step1))
            scores = jnp.exp(scores - highest)
            step0 = jnp.exp(step0 - highest)
            step1 = jnp.exp(step1 - highest)
            total = jnp.sum(scores, 1, keepdims=True) + step0 + step1
            raised.append((scores.astype(jnp.bfloat16), step0, step1, total))
        attended = []
        for here, (scores, step0, step1, total) in zip(pages, raised):
            values = r.pages[here, :, pl.ds(HEAD_DIM, HEAD_DIM)]
            attended.append(dot(scores, values.reshape(MAX_PAGES * PAGE, HEAD_DIM)))
        for at, index, values, (scores, step0, step1, total) in zip(
            lines, sequences, attended, raised
        ):
            values = values + step0 * r.seq_value[pl.ds(index, 1)]
            values = values + step1 * r.seq_value[pl.ds(dec_dev + index, 1)]
            r.seq_out[at, :] = values / total

    def visiting():
        swapped(visit_swap, r.visit_in.at[others])
        own = r.visit_out[pl.ds(pl.multiple_of(group * STEP_ROWS, STEP_ROWS), STEP_ROWS)]
        total = own.astype(jnp.float32)
        for step in range(1, GROUPS):
            total = total + r.visit_in[step].astype(jnp.float32)
        query = jnp.concatenate(
            [total[:, head * HEAD_DIM : (head + 1) * HEAD_DIM] for head in range(heads_dev)], 0
        ).astype(jnp.bfloat16)
        new_key = total[:, wide : wide + HEAD_DIM].astype(jnp.bfloat16)
        new_value = total[:, wide + HEAD_DIM :].astype(jnp.bfloat16)
        prior_scores = dot_rows(query, prior[:, pl.ds(0, HEAD_DIM)]) * scale + prior_bias[...]
        own_scores = dot_rows(query, r.pre_key[...]) * scale
        step_scores = dot_rows(query, new_key) * scale
        row = lax.broadcasted_iota(jnp.int32, step_scores.shape, 0) % STEP_ROWS
        column = lax.broadcasted_iota(jnp.int32, step_scores.shape, 1)
        step_scores = jnp.where((column <= row) & (column < 2), step_scores, masked_score)
        highest = jnp.maximum(
            jnp.max(prior_scores, 1, keepdims=True), jnp.max(own_scores, 1, keepdims=True)
        )
        highest = jnp.maximum(highest, jnp.max(step_scores, 1, keepdims=True))
        prior_raised = jnp.exp(prior_scores - highest)
        own_raised = jnp.exp(own_scores - highest)
        step_raised = jnp.exp(step_scores - highest)
        total = jnp.sum(prior_raised, 1, keepdims=True) + jnp.sum(own_raised, 1, keepdims=True)
        total = total + jnp.sum(step_raised, 1, keepdims=True)
        values = dot(prior_raised.astype(jnp.bfloat16), prior[:, pl.ds(HEAD_DIM, HEAD_DIM)])
        values = values + dot(own_raised.astype(jnp.bfloat16), pre_pair[1])
        values = values + dot(step_raised.astype(jnp.bfloat16), new_value)
        values = (values / total).astype(jnp.bfloat16)
        for head in range(heads_dev):
            r.taken_heads[group, :, pl.ds(head * HEAD_DIM, HEAD_DIM)] = values[
                head * STEP_ROWS : (head + 1) * STEP_ROWS
            ]
        for step in range(1, GROUPS):
            other = (group + step) % GROUPS
            swap(take_swap, r.taken_heads.at[group], r.taken_heads.at[group], {"grp": other})

    cached_some(0)
    pre_scatter.near_send(1)
    cached_some(1)
    cached_some(2)
    visiting()
    cached_some(3)
    pre_scatter.line_sum(2)
    pre_scatter.relay_send2()
    cached_some(4)
    cached_some(5)
    cached_some(6)
    cached_some(7)

    for head in range(heads_dev):
        lines = r.seq_out[pl.ds(head * rows, rows)].reshape(SPLIT, 2, dec_dev, HEAD_DIM)
        r.seq_back[:, :, :, pl.ds(head * HEAD_DIM, HEAD_DIM)] = lines.astype(jnp.bfloat16)
    dec_heads = r.dec_heads
    for t in (0, 1):
        swap(
            back_swap,
            r.seq_back.at[1 - member, t],
            dec_heads.at[of_member(t, member)],
            beside,
        )
        dec_heads[of_member(t, member)] = r.seq_back[member, t]
    pre_scatter.near_send(0)
    pre_scatter.line_sum(-1)
    pre_scatter.line_sum(1)
    pre_scatter.near_send2()
    swapped(take_swap, r.taken_heads.at[others])
    placed = lax.dot_general(
        r.picks[...],
        r.taken_heads[...].reshape(GROUPS * STEP_ROWS, wide),
        (((0,), (0,)), ((), ())),
        preferred_element_type=jnp.float32,
    )
    swapped(back_swap, r.seq_back.at[1 - member])
    taken = r.taken[:, 0:1] > 0.5
    r.dec_final[...] = jnp.where(taken, placed, dec_heads[...].astype(jnp.float32)).astype(
        jnp.bfloat16
    )
    dec_final, dec_terms = r.dec_final, r.dec_terms
    for index, ds in enumerate((2, -1, 1, 0)):
        terms(dec_final, dec_terms, ORDER[index])
        dec_scatter.relay_send(ds)
    dec_scatter.near_send(2)
    terms(dec_final, dec_terms, ORDER[4])
    dec_scatter.near_send(-1)
    dec_scatter.near_send(1)
    terms(dec_final, dec_terms, ORDER[5] + ORDER[6])
    pre_scatter.line_sum(0)
    pre_scatter.finish()
    pre_store = pltpu.make_async_copy(r.pre_result, r.pre_out, r.other_load.at[10])
    pre_store.start()
    dec_scatter.line_sum(2)
    dec_scatter.relay_send2()
    dec_scatter.near_send(0)
    dec_scatter.line_sum(-1)
    dec_scatter.line_sum(1)
    dec_scatter.near_send2()
    dec_scatter.line_sum(0)
    dec_scatter.finish()
    dec_store = pltpu.make_async_copy(r.dec_result, r.dec_out, r.other_load.at[11])
    dec_store.start()
    pre_store.wait()
    dec_store.wait()
    rest = pl.ds(1, BLOCKS - 1)
    pre.copies.sent(pre.held.at[rest])
    dec.copies.sent(dec.held.at[rest])
    pre_scatter.copies.sent(pre_terms.at[rest])
    dec_scatter.copies.sent(dec_terms.at[rest])
    for kind, region in (
        (pre_swap, pre_pair.at[member]),
        (dec_swap, dec_pair.at[member]),
        (query_swap, r.seq_query.at[member]),
        (visit_swap, r.visit_in.at[others]),
        (take_swap, r.taken_heads.at[others]),
        (back_swap, r.seq_back.at[member]),
    ):
        await_bytes(region, r.small_send.at[kind])


def scatter_scratch(rows, width):
    half, quarter = rows // 2, rows // 4
    return (
        pltpu.VMEM((BLOCKS, rows, width), jnp.bfloat16),
        pltpu.VMEM((2, RING, 2, quarter, width), jnp.bfloat16),
        pltpu.VMEM((2, RING, 2, half, width), jnp.bfloat16),
        pltpu.VMEM((2, 2, quarter, width), jnp.bfloat16),
        pltpu.VMEM((2, 2, half, width), jnp.bfloat16),
    )


def body(
    prefill_x,
    span_index,
    prefix_pages,
    prefix_cache,
    decode_x,
    decode_len,
    page_order,
    assignment,
    kv_cache,
    w_query,
    w_keyval,
    w_out,
):
    span, depth = prefill_x.shape
    decode = decode_x.shape[1]
    rows = 2 * decode
    dec_dev = decode // SPLIT
    wide = w_query.shape[1]
    both = wide + w_keyval.shape[1]
    carried = wide + 2 * HEAD_DIM
    pre_rows = prefix_cache.shape[2]
    pool_pages = page_order.shape[2]
    exponent = np.arange(HEAD_DIM, dtype=np.float64) % (HEAD_DIM // 2) * (2.0 / HEAD_DIM)
    frequency = (rope_base ** (-exponent)).astype(np.float32)[None, :]
    hbm = pl.BlockSpec(memory_space=pl.ANY)
    operands = dict(
        pre_x=(prefill_x, hbm),
        dec_x=(decode_x.reshape(rows, depth), hbm),
        frequency_hbm=(jnp.asarray(frequency), hbm),
        span_index_hbm=(span_index, hbm),
        assignment_hbm=(assignment, hbm),
        prefix_pages_hbm=(prefix_pages, hbm),
        decode_len_hbm=(decode_len, hbm),
        page_order_hbm=(page_order, hbm),
        w_query=(w_query, hbm),
        w_keyval=(w_keyval, hbm),
        w_out=(w_out, hbm),
        prior_hbm=(prefix_cache.reshape(pre_rows, 2 * HEAD_DIM), hbm),
        pool_hbm=(kv_cache.reshape(pool_pages, PAGE, 2 * HEAD_DIM), hbm),
    )
    results = dict(
        pre_out=jax.ShapeDtypeStruct((span, depth), jnp.bfloat16),
        dec_out=jax.ShapeDtypeStruct((rows, depth), jnp.bfloat16),
    )
    narrow, full = jnp.bfloat16, jnp.float32
    scratch = dict(
        frequency=pltpu.VMEM((1, HEAD_DIM), full),
        span_index=pltpu.SMEM(span_index.shape, jnp.int32),
        assignment=pltpu.SMEM(assignment.shape, jnp.int32),
        prefix_pages=pltpu.SMEM(prefix_pages.shape, jnp.int32),
        decode_len=pltpu.SMEM(decode_len.shape, jnp.int32),
        page_order=pltpu.SMEM(page_order.shape, jnp.int32),
        pre_result=pltpu.VMEM((span, depth), narrow),
        dec_result=pltpu.VMEM((rows, depth), narrow),
        pre_held=pltpu.VMEM((BLOCKS, span, depth), narrow),
        dec_held=pltpu.VMEM((BLOCKS, rows, depth), narrow),
        weights=pltpu.VMEM((BLOCKS, depth, both), narrow),
        out_weights=pltpu.VMEM((BLOCKS, wide, depth), narrow),
        pre_total=pltpu.VMEM((span, both), full),
        dec_total=pltpu.VMEM((rows, both), full),
        pool=pltpu.VMEM((pool_pages, PAGE, 2 * HEAD_DIM), narrow),
        pages=pltpu.VMEM((pool_pages + MAX_PAGES, PAGE, 2 * HEAD_DIM), narrow),
        prior=pltpu.VMEM((pre_rows, 2 * HEAD_DIM), narrow),
        prior_bias=pltpu.VMEM((1, pre_rows), full),
        pre_cos=pltpu.VMEM((span, HEAD_DIM), full),
        pre_sin=pltpu.VMEM((span, HEAD_DIM), full),
        dec_cos=pltpu.VMEM((rows, HEAD_DIM), full),
        dec_sin=pltpu.VMEM((rows, HEAD_DIM), full),
        taken=pltpu.VMEM((rows, HEAD_DIM), full),
        picks=pltpu.VMEM((GROUPS * STEP_ROWS, rows), narrow),
        pre_pair=pltpu.VMEM((SPLIT, span, HEAD_DIM), narrow),
        dec_pair=pltpu.VMEM((SPLIT, rows, HEAD_DIM), narrow),
        pre_query=pltpu.VMEM((span, wide), narrow),
        pre_key=pltpu.VMEM((span, HEAD_DIM), narrow),
        pre_heads=pltpu.VMEM((span, wide), narrow),
        steps=pltpu.VMEM((rows, carried), narrow),
        seq_query=pltpu.VMEM((SPLIT, 2, dec_dev, wide), narrow),
        seq_rows=pltpu.VMEM((rows * wide // HEAD_DIM, HEAD_DIM), full),
        seq_key=pltpu.VMEM((2 * dec_dev, HEAD_DIM), full),
        seq_value=pltpu.VMEM((2 * dec_dev, HEAD_DIM), full),
        seq_out=pltpu.VMEM((rows * wide // HEAD_DIM, HEAD_DIM), full),
        seq_back=pltpu.VMEM((SPLIT, 2, dec_dev, wide), narrow),
        dec_heads=pltpu.VMEM((rows, wide), narrow),
        dec_final=pltpu.VMEM((rows, wide), narrow),
        visit_out=pltpu.VMEM((GROUPS * STEP_ROWS, carried), narrow),
        visit_in=pltpu.VMEM((GROUPS, STEP_ROWS, carried), narrow),
        taken_heads=pltpu.VMEM((GROUPS, STEP_ROWS, wide), narrow),
        **dict(zip(("pre_terms", "pre_relays", "pre_halves", "pre_relay2", "pre_halves2"), scatter_scratch(span, depth))),
        **dict(zip(("dec_terms", "dec_relays", "dec_halves", "dec_relay2", "dec_halves2"), scatter_scratch(rows, depth))),
        load=pltpu.SemaphoreType.DMA((BLOCKS,)),
        out_load=pltpu.SemaphoreType.DMA((BLOCKS,)),
        other_load=pltpu.SemaphoreType.DMA((12,)),
        send=pltpu.SemaphoreType.DMA((4,)),
        gather_receive=pltpu.SemaphoreType.DMA((2, 30)),
        scatter_receive=pltpu.SemaphoreType.DMA((2, 20)),
        small_send=pltpu.SemaphoreType.DMA((6,)),
        small_receive=pltpu.SemaphoreType.DMA((6,)),
    )
    names = tuple(operands) + tuple(results) + tuple(scratch)
    prefill_out, decode_out = pl.pallas_call(
        functools.partial(layer_kernel, names),
        out_shape=tuple(results.values()),
        in_specs=[spec for _, spec in operands.values()],
        out_specs=(hbm, hbm),
        scratch_shapes=list(scratch.values()),
        compiler_params=pltpu.CompilerParams(
            collective_id=0, has_side_effects=True, vmem_limit_bytes=60 * 2**20
        ),
        name="layer",
    )(*(value for value, _ in operands.values()))
    return (prefill_out, decode_out.reshape(2, decode, -1))


def solution(mesh):
    placed = (
        P("grp", "tp"),
        P(),
        P("grp", None),
        P("grp", "tp", None, None),
        P(None, "grp", "tp"),
        P("grp", None, None),
        P("grp", None, None),
        P(),
        P("grp", "tp", None, None),
        P(None, "tp"),
        P(None, "tp"),
        P("tp", None),
    )
    return jax.shard_map(
        body,
        mesh=mesh,
        in_specs=placed,
        out_specs=(P("grp", "tp"), P(None, "grp", "tp")),
        check_vma=False,
    )
```

```python
import functools
import types

import jax
import jax.numpy as jnp
import numpy as np
from jax import lax
from jax.experimental import pallas as pl
from jax.experimental.pallas import tpu as pltpu
from jax.sharding import PartitionSpec as P

KV_HEADS = 8
HEAD_DIM = 128
SPANS = 8
PAGE = 16
MAX_PAGES = 32
RING = 4
BLOCKS = RING * RING
SPLIT = 2
GROUPS = 8
STEP_ROWS = 16
MESH = pl.DeviceIdType.MESH

rope_base = 500000.0
masked_score = -1e30


def place(dz, dx):
    return (dz % RING) * RING + dx % RING


def neighbours():
    me = lax.axis_index("tp")
    z = me // RING
    x = me % RING
    return {
        ("z", 1): ((z + 1) % RING) * RING + x,
        ("z", -1): ((z + RING - 1) % RING) * RING + x,
        ("x", 1): z * RING + (x + 1) % RING,
        ("x", -1): z * RING + (x + RING - 1) % RING,
    }


def absolute(dz, dx):
    me = lax.axis_index("tp")
    z = me // RING
    x = me % RING
    return ((z + dz) % RING) * RING + (x + dx) % RING


def axes_of(half, first):
    return ("x", "z") if (half == 0) == first else ("z", "x")


def await_bytes(region, semaphore):
    pltpu.make_async_copy(region, region, semaphore).wait()


class Copies:
    def __init__(self, near, send, receive):
        self.near, self.send, self.receive = near, send, receive
        self.index = {}

    def start(self, name, axis, step, source, target):
        index = self.index.setdefault(name, len(self.index))
        pltpu.make_async_remote_copy(
            src_ref=source,
            dst_ref=target,
            send_sem=self.send,
            recv_sem=self.receive.at[index],
            device_id={"tp": self.near[axis, step]},
            device_id_type=MESH,
        ).start()

    def arrive(self, name, region):
        await_bytes(region, self.receive.at[self.index[name]])

    def sent(self, region):
        await_bytes(region, self.send)


class Gather:
    def __init__(self, own, held, copies):
        self.own, self.held, self.copies = own, held, copies
        self.rows = own.shape[0]

    def slot(self, half, d1, d2):
        return place(d2, d1) if half == 0 else place(d1, d2)

    def part(self, half, d1, d2, quarter=None):
        count = self.rows // 2
        first = half * count
        if quarter is not None:
            count = count // 2
            first = first + quarter * count
        return self.held.at[self.slot(half, d1, d2), pl.ds(first, count)]

    def mine(self, half):
        count = self.rows // 2
        return self.held.at[0, pl.ds(half * count, count)]

    def first_sends(self):
        for half in (0, 1):
            axis = axes_of(half, True)[0]
            for step in (1, -1):
                self.copies.start(
                    ("1", half, step), axis, step, self.mine(half), self.part(half, -step, 0)
                )
        self.second_sends(0)

    def second_sends(self, d1):
        for half in (0, 1):
            self.second_send(half, d1)

    def second_send(self, half, d1):
        axis = axes_of(half, True)[1]
        for step in (1, -1):
            self.copies.start(
                ("2", half, d1, step),
                axis,
                step,
                self.part(half, d1, 0) if d1 != 0 else self.mine(half),
                self.part(half, d1, -step),
            )

    def near_arrive(self):
        for half in (0, 1):
            axis = axes_of(half, True)[0]
            for step in (1, -1):
                quarter = 0 if step == 1 else 1
                self.copies.arrive(("1", half, step), self.part(half, -step, 0))
                self.copies.start(
                    ("1f", half),
                    axis,
                    step,
                    self.part(half, -step, 0, quarter),
                    self.part(half, -2 * step, 0, quarter),
                )
                self.second_send(half, -step)
        return [(half, d1, 0) for half in (0, 1) for d1 in (-1, 1)]

    def far_arrive(self):
        for half in (0, 1):
            self.copies.arrive(("1f", half), self.part(half, 2, 0))
            self.second_send(half, 2)
        return [(half, 2, 0) for half in (0, 1)]

    def line_arrive(self, d1):
        for half in (0, 1):
            axis = axes_of(half, True)[1]
            for step in (1, -1):
                quarter = 0 if step == 1 else 1
                self.copies.arrive(("2", half, d1, step), self.part(half, d1, -step))
                self.copies.start(
                    ("2f", half, d1),
                    axis,
                    step,
                    self.part(half, d1, -step, quarter),
                    self.part(half, d1, -2 * step, quarter),
                )
        return [(half, d1, d2) for half in (0, 1) for d2 in (-1, 1)]

    def last_arrive(self, d1):
        for half in (0, 1):
            self.copies.arrive(("2f", half, d1), self.part(half, d1, 2))
        return [(half, d1, 2) for half in (0, 1)]


class Scatter:
    def __init__(self, terms, relays, halves, relay2, halves2, out, copies):
        self.terms, self.relays, self.halves = terms, relays, halves
        self.relay2, self.halves2, self.out, self.copies = relay2, halves2, out, copies
        self.rows = terms.shape[1]

    def part(self, half, df, ds, quarter=None):
        count = self.rows // 2
        first = half * count
        if quarter is not None:
            count = count // 2
            first = first + quarter * count
        slot = place(df, ds) if half == 0 else place(ds, df)
        return self.terms.at[slot, pl.ds(first, count)]

    def relay_send(self, ds):
        for half in (0, 1):
            axis = axes_of(half, False)[0]
            for quarter, step in ((0, 1), (1, -1)):
                self.copies.start(
                    ("1r", half, ds),
                    axis,
                    step,
                    self.part(half, 2, ds, quarter),
                    self.relays.at[half, ds % RING, quarter],
                )

    def near_send(self, ds):
        for half in (0, 1):
            axis = axes_of(half, False)[0]
            self.copies.arrive(("1r", half, ds), self.relays.at[half, ds % RING])
            for quarter, step in ((0, 1), (1, -1)):
                own = self.part(half, step, ds, quarter)
                added = self.relays[half, ds % RING, quarter].astype(jnp.float32)
                own[...] = (own[...].astype(jnp.float32) + added).astype(jnp.bfloat16)
                self.copies.start(
                    ("1", half, ds),
                    axis,
                    step,
                    self.part(half, step, ds),
                    self.halves.at[half, ds % RING, quarter],
                )

    def line_sum(self, ds):
        for half in (0, 1):
            self.copies.arrive(("1", half, ds), self.halves.at[half, ds % RING])
            own = self.part(half, 0, ds)
            total = own[...].astype(jnp.float32)
            for side in (0, 1):
                total = total + self.halves[half, ds % RING, side].astype(jnp.float32)
            own[...] = total.astype(jnp.bfloat16)

    def relay_send2(self):
        for half in (0, 1):
            axis = axes_of(half, False)[1]
            for quarter, step in ((0, 1), (1, -1)):
                self.copies.start(
                    ("2r", half),
                    axis,
                    step,
                    self.part(half, 0, 2, quarter),
                    self.relay2.at[half, quarter],
                )

    def near_send2(self):
        for half in (0, 1):
            axis = axes_of(half, False)[1]
            self.copies.arrive(("2r", half), self.relay2.at[half])
            for quarter, step in ((0, 1), (1, -1)):
                own = self.part(half, 0, step, quarter)
                added = self.relay2[half, quarter].astype(jnp.float32)
                own[...] = (own[...].astype(jnp.float32) + added).astype(jnp.bfloat16)
                self.copies.start(
                    ("2", half),
                    axis,
                    step,
                    self.part(half, 0, step),
                    self.halves2.at[half, quarter],
                )

    def finish(self):
        count = self.rows // 2
        for half in (0, 1):
            self.copies.arrive(("2", half), self.halves2.at[half])
            total = self.part(half, 0, 0)[...].astype(jnp.float32)
            for side in (0, 1):
                total = total + self.halves2[half, side].astype(jnp.float32)
            self.out[pl.ds(half * count, count)] = total.astype(jnp.bfloat16)


def partner():
    me = lax.axis_index("tp")
    return me + 1 - 2 * (me % SPLIT)


def greet_all(near):
    barrier = pltpu.get_barrier_semaphore()
    group = lax.axis_index("grp")
    for device in near.values():
        pl.semaphore_signal(barrier, inc=1, device_id={"tp": device}, device_id_type=MESH)
    for step in range(1, GROUPS):
        other = (group + step) % GROUPS
        pl.semaphore_signal(barrier, inc=1, device_id={"grp": other}, device_id_type=MESH)
    pl.semaphore_wait(barrier, len(near) + GROUPS - 1)


ORDER = (
    ((2, 2),),
    ((2, -1), (-1, 2)),
    ((2, 1), (1, 2)),
    ((2, 0), (0, 2)),
    ((-1, -1), (-1, 1), (1, -1), (1, 1)),
    ((-1, 0), (1, 0), (0, -1), (0, 1)),
    ((0, 0),),
)


def lane_turn(values):
    half = HEAD_DIM // 2
    return jnp.concatenate([values[:, half:], values[:, :half]], 1)


def turn_tables(positions, frequency):
    angles = positions * frequency
    lanes = lax.broadcasted_iota(jnp.int32, angles.shape, 1)
    sine = jnp.sin(angles)
    return jnp.cos(angles), jnp.where(lanes < HEAD_DIM // 2, -sine, sine)


def turn(values, cosine, sine):
    return (values * cosine + lane_turn(values) * sine).astype(jnp.bfloat16)


def dot_rows(left, right):
    return lax.dot_general(
        left, right, (((1,), (1,)), ((), ())), preferred_element_type=jnp.float32
    )


def dot(left, right):
    return jnp.dot(left, right, preferred_element_type=jnp.float32)


def layer_kernel(names, *refs):
    r = types.SimpleNamespace(**dict(zip(names, refs)))
    near = neighbours()
    me = lax.axis_index("tp")
    group = lax.axis_index("grp")
    member = me % SPLIT
    pre_x, dec_x = r.pre_x, r.dec_x
    span, depth = pre_x.shape
    rows = dec_x.shape[0]
    decode = rows // 2
    dec_dev = decode // SPLIT
    wide = r.w_query.shape[1]
    heads_dev = wide // HEAD_DIM
    pre_rows = r.prior_hbm.shape[0]
    pool_pages = r.pool_hbm.shape[0]
    scale = HEAD_DIM ** (-0.5)

    loads, out_loads = {}, {}
    order = ((0, 0), (0, -1), (0, 1), (-1, 0), (1, 0), (0, 2), (2, 0), (-1, -1), (-1, 1), (1, -1))
    order += ((1, 1), (2, -1), (2, 1), (-1, 2), (1, 2), (2, 2))
    order = [place(*offset) for offset in order]
    weights, out_weights = r.weights, r.out_weights
    for slot in order:
        origin = absolute(slot // RING, slot % RING)
        span_rows = pl.ds(pl.multiple_of(origin * depth, depth), depth)
        loads[slot] = (
            pltpu.make_async_copy(
                r.w_query.at[span_rows],
                weights.at[slot, :, pl.ds(0, wide)],
                r.load.at[slot],
            ),
            pltpu.make_async_copy(
                r.w_keyval.at[span_rows],
                weights.at[slot, :, pl.ds(wide, HEAD_DIM)],
                r.load.at[slot],
            ),
        )
    for slot in order:
        origin = absolute(slot // RING, slot % RING)
        columns = pl.ds(pl.multiple_of(origin * depth, depth), depth)
        out_loads[slot] = pltpu.make_async_copy(
            r.w_out.at[:, columns], out_weights.at[slot], r.out_load.at[slot]
        )
    prior_load = pltpu.make_async_copy(r.prior_hbm, r.prior, r.other_load.at[0])
    pre_load = pltpu.make_async_copy(pre_x, r.pre_held.at[0], r.other_load.at[1])
    dec_load = pltpu.make_async_copy(dec_x, r.dec_held.at[0], r.other_load.at[2])
    pool_loads = []
    for part in range(4):
        pages = pl.ds(part * pool_pages // 4, pool_pages // 4)
        pool_loads.append(
            pltpu.make_async_copy(r.pool_hbm.at[pages], r.pool.at[pages], r.other_load.at[3])
        )
    small_loads = [
        pltpu.make_async_copy(source, target, r.other_load.at[4 + index])
        for index, (source, target) in enumerate(
            (
                (r.span_index_hbm, r.span_index),
                (r.assignment_hbm, r.assignment),
                (r.frequency_hbm, r.frequency),
                (r.prefix_pages_hbm, r.prefix_pages),
                (r.decode_len_hbm, r.decode_len),
                (r.page_order_hbm, r.page_order),
            )
        )
    ]
    pre_load.start()
    dec_load.start()
    for copy in small_loads:
        copy.start()
    for slot in order[:5]:
        for copy in loads[slot]:
            copy.start()
    waiting = [copy for slot in order[5:] for copy in loads[slot]]
    waiting += pool_loads + [prior_load] + [out_loads[place(*d)] for d in sum(ORDER, ())]

    def load_more(count):
        for copy in waiting[:count]:
            copy.start()
        del waiting[:count]

    greet_all(near)
    loaded = set()

    def multiply(gather, total, parts):
        for half, d1, d2 in parts:
            slot = gather.slot(half, d1, d2)
            if slot not in loaded:
                loaded.add(slot)
                await_bytes(weights.at[slot], r.load.at[slot])
            count = gather.rows // 2
            at = pl.ds(half * count, count)
            product = dot(gather.part(half, d1, d2)[...], weights[slot])
            if slot == 0:
                total[at] = product
            else:
                total[at] += product

    pre = Gather(pre_x, r.pre_held, Copies(near, r.send.at[0], r.gather_receive.at[0]))
    dec = Gather(dec_x, r.dec_held, Copies(near, r.send.at[1], r.gather_receive.at[1]))
    pre_total, dec_total = r.pre_total, r.dec_total
    pre_load.wait()
    pre.first_sends()
    load_more(4)
    multiply(pre, pre_total, [(0, 0, 0), (1, 0, 0)])

    for copy in small_loads:
        copy.wait()

    span_of = [r.span_index[s] for s in range(GROUPS)]
    goes_to = [r.assignment[s] for s in range(GROUPS)]
    to_here, owner = [], []
    rank = 0 * group
    for s in range(GROUPS):
        here = jnp.where((span_of[s] == SPANS - 1) & (goes_to[s] == group), 1, 0)
        to_here.append(here)
        owner.append((rank & 1) * dec_dev + (rank >> 1))
        rank = rank + here
    start_row = r.span_index[group] * span
    frequency = r.frequency[...]

    def prior_mask():
        live_pages = start_row // PAGE
        column_page = lax.broadcasted_iota(jnp.int32, (1, pre_rows), 1) // PAGE

        def mark(index, live):
            page = r.prefix_pages[0, index]
            page = jnp.where(index < live_pages, page, -1)
            return jnp.where(column_page == page, 0.0, live)

        live = jnp.full((1, pre_rows), masked_score, jnp.float32)
        r.prior_bias[...] = lax.fori_loop(0, pre_rows // PAGE, mark, live, unroll=8)

    def pre_tables():
        spots = (start_row + lax.broadcasted_iota(jnp.int32, (span, HEAD_DIM), 0)).astype(
            jnp.float32
        )
        cosine, sine = turn_tables(spots, frequency)
        r.pre_cos[...] = cosine
        r.pre_sin[...] = sine

    def dec_tables():
        row = lax.broadcasted_iota(jnp.int32, (rows, HEAD_DIM), 0)
        sequence = row % decode

        def spread(index, base):
            length = r.decode_len[0, index // dec_dev, index % dec_dev]
            return jnp.where(sequence == index, length, base)

        base = lax.fori_loop(0, decode, spread, jnp.zeros_like(row), unroll=4)
        taken = jnp.zeros(row.shape, jnp.float32)
        for s in range(GROUPS):
            mine = jnp.where(to_here[s] == 1, owner[s], -1)
            taken = jnp.where(sequence == mine, 1.0, taken)
        base = jnp.where(taken > 0.5, pre_rows + span, base)
        cosine, sine = turn_tables((base + row // decode).astype(jnp.float32), frequency)
        r.dec_cos[...] = cosine
        r.dec_sin[...] = sine
        r.taken[...] = taken
        row = lax.broadcasted_iota(jnp.int32, (STEP_ROWS, rows), 0)
        column = lax.broadcasted_iota(jnp.int32, (STEP_ROWS, rows), 1)
        for s in range(GROUPS):
            mine = jnp.where(to_here[s] == 1, owner[s], -rows)
            picked = (column == row * decode + mine) & (row < 2)
            r.picks[pl.ds(s * STEP_ROWS, STEP_ROWS)] = jnp.where(picked, 1.0, 0.0).astype(
                jnp.bfloat16
            )

    pieces = 8
    chunk = pool_pages // pieces

    def reorder(piece):
        def move(index, carry):
            page = r.page_order[0, member, index]
            r.pages[index] = r.pool[page]
            return carry

        lax.fori_loop(piece * chunk, (piece + 1) * chunk, move, 0, unroll=4)

    pre_tables()
    load_more(6)
    multiply(pre, pre_total, pre.near_arrive())
    prior_mask()
    load_more(6)
    multiply(pre, pre_total, pre.far_arrive())
    dec_tables()
    for d1 in (0, -1, 1, 2):
        parts = pre.line_arrive(d1)
        load_more(4)
        if d1 == 2:
            dec_load.wait()
            dec.first_sends()
        multiply(pre, pre_total, parts)
    multiply(dec, dec_total, [(0, 0, 0), (1, 0, 0)])
    await_bytes(r.pool, r.other_load.at[3])
    r.pages[pl.ds(pool_pages, MAX_PAGES)] = jnp.zeros(
        (MAX_PAGES, PAGE, 2 * HEAD_DIM), jnp.bfloat16
    )
    for index, d1 in enumerate((0, -1, 1, 2)):
        multiply(pre, pre_total, pre.last_arrive(d1))
        load_more(3)
        reorder(2 * index)
        reorder(2 * index + 1)
    load_more(len(waiting))

    def swap(kind, source, target, device):
        pltpu.make_async_remote_copy(
            src_ref=source,
            dst_ref=target,
            send_sem=r.small_send.at[kind],
            recv_sem=r.small_receive.at[kind],
            device_id=device,
            device_id_type=MESH,
        ).start()

    def swapped(kind, region):
        await_bytes(region, r.small_receive.at[kind])

    pre_swap, dec_swap, query_swap, visit_swap, take_swap, back_swap = range(6)
    others = pl.ds(1, GROUPS - 1)
    beside = {"tp": partner()}
    pre_pair, dec_pair = r.pre_pair, r.dec_pair
    pre_pair[member] = pre_total[:, wide:].astype(jnp.bfloat16)
    swap(pre_swap, pre_pair.at[member], pre_pair.at[member], beside)
    cosine, sine = r.pre_cos[...], r.pre_sin[...]
    for head in range(heads_dev):
        at = pl.ds(head * HEAD_DIM, HEAD_DIM)
        r.pre_query[:, at] = turn(pre_total[:, at], cosine, sine)
    dec_parts = dec.near_arrive()
    multiply(dec, dec_total, dec_parts)
    swapped(pre_swap, pre_pair.at[1 - member])
    r.pre_key[...] = turn(
        pre_pair[0].astype(jnp.float32), r.pre_cos[...], r.pre_sin[...]
    )
    prior_load.wait()
    prior_bias = r.prior_bias
    prior = r.prior
    block = span // 2

    def attend(head, part):
        at = pl.ds(head * HEAD_DIM, HEAD_DIM)
        here = pl.ds(part * block, block)
        query = r.pre_query[here, at]
        prior_scores = dot_rows(query, prior[:, pl.ds(0, HEAD_DIM)]) * scale + prior_bias[...]
        own_scores = dot_rows(query, r.pre_key[...]) * scale
        row = lax.broadcasted_iota(jnp.int32, own_scores.shape, 0) + part * block
        column = lax.broadcasted_iota(jnp.int32, own_scores.shape, 1)
        own_scores = jnp.where(row >= column, own_scores, masked_score)
        highest = jnp.maximum(
            jnp.max(prior_scores, 1, keepdims=True), jnp.max(own_scores, 1, keepdims=True)
        )
        prior_raised = jnp.exp(prior_scores - highest)
        own_raised = jnp.exp(own_scores - highest)
        total = jnp.sum(prior_raised, 1, keepdims=True) + jnp.sum(own_raised, 1, keepdims=True)
        values = dot(prior_raised.astype(jnp.bfloat16), prior[:, pl.ds(HEAD_DIM, HEAD_DIM)])
        values = values + dot(own_raised.astype(jnp.bfloat16), pre_pair[1])
        r.pre_heads[here, at] = (values / total).astype(jnp.bfloat16)

    def terms(heads, kept, blocks):
        for dz, dx in blocks:
            slot = place(dz, dx)
            if slot not in term_loaded:
                term_loaded.add(slot)
                out_loads[slot].wait()
            kept[slot] = dot(heads[...], out_weights[slot]).astype(jnp.bfloat16)

    term_loaded = set()
    pre_scatter = Scatter(
        r.pre_terms,
        r.pre_relays,
        r.pre_halves,
        r.pre_relay2,
        r.pre_halves2,
        r.pre_result,
        Copies(near, r.send.at[2], r.scatter_receive.at[0]),
    )
    dec_scatter = Scatter(
        r.dec_terms,
        r.dec_relays,
        r.dec_halves,
        r.dec_relay2,
        r.dec_halves2,
        r.dec_result,
        Copies(near, r.send.at[3], r.scatter_receive.at[1]),
    )
    pre_heads, pre_terms = r.pre_heads, r.pre_terms
    work = [(head, part) for head in range(heads_dev) for part in (0, 1)]
    events = [dec.far_arrive]
    events += [functools.partial(dec.line_arrive, d1) for d1 in (0, -1, 1, 2)]
    for index, item in enumerate(work):
        if index < len(events):
            multiply(dec, dec_total, events[index]())
        attend(*item)
    for d1 in (0, -1, 1, 2):
        if d1 == 1:
            terms(pre_heads, pre_terms, ORDER[0])
            pre_scatter.relay_send(2)
            terms(pre_heads, pre_terms, ORDER[1])
            pre_scatter.relay_send(-1)
        multiply(dec, dec_total, dec.last_arrive(d1))

    dec_pair[member] = dec_total[:, wide:].astype(jnp.bfloat16)
    swap(dec_swap, dec_pair.at[member], dec_pair.at[member], beside)
    cosine, sine = r.dec_cos[...], r.dec_sin[...]
    for head in range(heads_dev):
        at = pl.ds(head * HEAD_DIM, HEAD_DIM)
        r.steps[:, at] = turn(dec_total[:, at], cosine, sine)

    def of_member(t, which):
        return pl.ds(pl.multiple_of(t * decode + which * dec_dev, dec_dev), dec_dev)

    for t in (0, 1):
        swap(
            query_swap,
            r.steps.at[of_member(t, 1 - member), pl.ds(0, wide)],
            r.seq_query.at[member, t],
            beside,
        )
        r.seq_query[member, t] = r.steps[of_member(t, member), pl.ds(0, wide)]

    terms(pre_heads, pre_terms, ORDER[2])
    pre_scatter.relay_send(1)
    terms(pre_heads, pre_terms, ORDER[3])
    pre_scatter.relay_send(0)
    pre_scatter.near_send(2)
    terms(pre_heads, pre_terms, ORDER[4])

    swapped(dec_swap, dec_pair.at[1 - member])
    r.steps[:, pl.ds(wide, HEAD_DIM)] = turn(
        dec_pair[0].astype(jnp.float32), r.dec_cos[...], r.dec_sin[...]
    )
    r.steps[:, pl.ds(wide + HEAD_DIM, HEAD_DIM)] = dec_pair[1]
    r.visit_out[...] = dot(r.picks[...], r.steps[...]).astype(jnp.bfloat16)
    for step in range(1, GROUPS):
        other = (group + step) % GROUPS
        here = pl.ds(pl.multiple_of(other * STEP_ROWS, STEP_ROWS), STEP_ROWS)
        swap(visit_swap, r.visit_out.at[here], r.visit_in.at[step], {"grp": other})
    for t in (0, 1):
        here = pl.ds(t * dec_dev, dec_dev)
        r.seq_key[here] = r.steps[of_member(t, member), pl.ds(wide, HEAD_DIM)].astype(
            jnp.float32
        )
        r.seq_value[here] = r.steps[
            of_member(t, member), pl.ds(wide + HEAD_DIM, HEAD_DIM)
        ].astype(jnp.float32)
    pre_scatter.near_send(-1)
    swapped(query_swap, r.seq_query.at[1 - member])
    for head in range(heads_dev):
        lines = r.seq_query[:, :, :, pl.ds(head * HEAD_DIM, HEAD_DIM)]
        r.seq_rows[pl.ds(head * rows, rows)] = lines.reshape(rows, HEAD_DIM).astype(jnp.float32)

    counts = [
        (r.decode_len[0, member, index] + (PAGE - 1)) >> 4 for index in range(dec_dev)
    ]
    firsts, total_pages = [], 0
    for index in range(dec_dev):
        firsts.append(total_pages)
        total_pages = total_pages + counts[index]

    def cached_some(part):
        sequences = range(part * dec_dev // 8, (part + 1) * dec_dev // 8)
        lines = [pl.ds(index, 2 * SPLIT * heads_dev, stride=dec_dev) for index in sequences]
        pages = [pl.ds(firsts[index], MAX_PAGES) for index in sequences]
        found = []
        for at, index, here in zip(lines, sequences, pages):
            query = r.seq_rows[at, :]
            keys = r.pages[here, :, pl.ds(0, HEAD_DIM)].reshape(MAX_PAGES * PAGE, HEAD_DIM)
            scores = dot_rows(query.astype(jnp.bfloat16), keys) * scale
            column = lax.broadcasted_iota(jnp.int32, scores.shape, 1)
            scores = jnp.where(column < r.decode_len[0, member, index], scores, masked_score)
            step0 = jnp.sum(query * r.seq_key[pl.ds(index, 1)], 1, keepdims=True) * scale
            step1 = jnp.sum(query * r.seq_key[pl.ds(dec_dev + index, 1)], 1, keepdims=True) * scale
            found.append((scores, step0, step1))
        raised = []
        for scores, step0, step1 in found:
            second = lax.broadcasted_iota(jnp.int32, step1.shape, 0) % 2 == 1
            step1 = jnp.where(second, step1, masked_score)
            highest = jnp.maximum(jnp.max(scores, 1, keepdims=True), jnp.maximum(step0, step1))
            scores = jnp.exp(scores - highest)
            step0 = jnp.exp(step0 - highest)
            step1 = jnp.exp(step1 - highest)
            total = jnp.sum(scores, 1, keepdims=True) + step0 + step1
            raised.append((scores.astype(jnp.bfloat16), step0, step1, total))
        attended = []
        for here, (scores, step0, step1, total) in zip(pages, raised):
            values = r.pages[here, :, pl.ds(HEAD_DIM, HEAD_DIM)]
            attended.append(dot(scores, values.reshape(MAX_PAGES * PAGE, HEAD_DIM)))
        for at, index, values, (scores, step0, step1, total) in zip(
            lines, sequences, attended, raised
        ):
            values = values + step0 * r.seq_value[pl.ds(index, 1)]
            values = values + step1 * r.seq_value[pl.ds(dec_dev + index, 1)]
            r.seq_out[at, :] = values / total

    def visiting():
        swapped(visit_swap, r.visit_in.at[others])
        own = r.visit_out[pl.ds(pl.multiple_of(group * STEP_ROWS, STEP_ROWS), STEP_ROWS)]
        total = own.astype(jnp.float32)
        for step in range(1, GROUPS):
            total = total + r.visit_in[step].astype(jnp.float32)
        query = jnp.concatenate(
            [total[:, head * HEAD_DIM : (head + 1) * HEAD_DIM] for head in range(heads_dev)], 0
        ).astype(jnp.bfloat16)
        new_key = total[:, wide : wide + HEAD_DIM].astype(jnp.bfloat16)
        new_value = total[:, wide + HEAD_DIM :].astype(jnp.bfloat16)
        prior_scores = dot_rows(query, prior[:, pl.ds(0, HEAD_DIM)]) * scale + prior_bias[...]
        own_scores = dot_rows(query, r.pre_key[...]) * scale
        step_scores = dot_rows(query, new_key) * scale
        row = lax.broadcasted_iota(jnp.int32, step_scores.shape, 0) % STEP_ROWS
        column = lax.broadcasted_iota(jnp.int32, step_scores.shape, 1)
        step_scores = jnp.where((column <= row) & (column < 2), step_scores, masked_score)
        highest = jnp.maximum(
            jnp.max(prior_scores, 1, keepdims=True), jnp.max(own_scores, 1, keepdims=True)
        )
        highest = jnp.maximum(highest, jnp.max(step_scores, 1, keepdims=True))
        prior_raised = jnp.exp(prior_scores - highest)
        own_raised = jnp.exp(own_scores - highest)
        step_raised = jnp.exp(step_scores - highest)
        total = jnp.sum(prior_raised, 1, keepdims=True) + jnp.sum(own_raised, 1, keepdims=True)
        total = total + jnp.sum(step_raised, 1, keepdims=True)
        values = dot(prior_raised.astype(jnp.bfloat16), prior[:, pl.ds(HEAD_DIM, HEAD_DIM)])
        values = values + dot(own_raised.astype(jnp.bfloat16), pre_pair[1])
        values = values + dot(step_raised.astype(jnp.bfloat16), new_value)
        values = (values / total).astype(jnp.bfloat16)
        for head in range(heads_dev):
            r.taken_heads[group, :, pl.ds(head * HEAD_DIM, HEAD_DIM)] = values[
                head * STEP_ROWS : (head + 1) * STEP_ROWS
            ]
        for step in range(1, GROUPS):
            other = (group + step) % GROUPS
            swap(take_swap, r.taken_heads.at[group], r.taken_heads.at[group], {"grp": other})

    cached_some(0)
    pre_scatter.near_send(1)
    cached_some(1)
    terms(pre_heads, pre_terms, ORDER[5] + ORDER[6])
    cached_some(2)
    visiting()
    cached_some(3)
    pre_scatter.line_sum(2)
    pre_scatter.relay_send2()
    cached_some(4)
    cached_some(5)
    cached_some(6)
    cached_some(7)

    for head in range(heads_dev):
        lines = r.seq_out[pl.ds(head * rows, rows)].reshape(SPLIT, 2, dec_dev, HEAD_DIM)
        r.seq_back[:, :, :, pl.ds(head * HEAD_DIM, HEAD_DIM)] = lines.astype(jnp.bfloat16)
    dec_heads = r.dec_heads
    for t in (0, 1):
        swap(
            back_swap,
            r.seq_back.at[1 - member, t],
            dec_heads.at[of_member(t, member)],
            beside,
        )
        dec_heads[of_member(t, member)] = r.seq_back[member, t]
    pre_scatter.near_send(0)
    pre_scatter.line_sum(-1)
    pre_scatter.line_sum(1)
    pre_scatter.near_send2()
    swapped(take_swap, r.taken_heads.at[others])
    placed = lax.dot_general(
        r.picks[...],
        r.taken_heads[...].reshape(GROUPS * STEP_ROWS, wide),
        (((0,), (0,)), ((), ())),
        preferred_element_type=jnp.float32,
    )
    swapped(back_swap, r.seq_back.at[1 - member])
    taken = r.taken[:, 0:1] > 0.5
    r.dec_final[...] = jnp.where(taken, placed, dec_heads[...].astype(jnp.float32)).astype(
        jnp.bfloat16
    )
    dec_final, dec_terms = r.dec_final, r.dec_terms
    for index, ds in enumerate((2, -1, 1, 0)):
        terms(dec_final, dec_terms, ORDER[index])
        dec_scatter.relay_send(ds)
    dec_scatter.near_send(2)
    terms(dec_final, dec_terms, ORDER[4])
    dec_scatter.near_send(-1)
    dec_scatter.near_send(1)
    terms(dec_final, dec_terms, ORDER[5] + ORDER[6])
    pre_scatter.line_sum(0)
    pre_scatter.finish()
    pre_store = pltpu.make_async_copy(r.pre_result, r.pre_out, r.other_load.at[10])
    pre_store.start()
    dec_scatter.line_sum(2)
    dec_scatter.relay_send2()
    dec_scatter.near_send(0)
    dec_scatter.line_sum(-1)
    dec_scatter.line_sum(1)
    dec_scatter.near_send2()
    dec_scatter.line_sum(0)
    dec_scatter.finish()
    dec_store = pltpu.make_async_copy(r.dec_result, r.dec_out, r.other_load.at[11])
    dec_store.start()
    pre_store.wait()
    dec_store.wait()
    rest = pl.ds(1, BLOCKS - 1)
    pre.copies.sent(pre.held.at[rest])
    dec.copies.sent(dec.held.at[rest])
    pre_scatter.copies.sent(pre_terms.at[rest])
    dec_scatter.copies.sent(dec_terms.at[rest])
    for kind, region in (
        (pre_swap, pre_pair.at[member]),
        (dec_swap, dec_pair.at[member]),
        (query_swap, r.seq_query.at[member]),
        (visit_swap, r.visit_in.at[others]),
        (take_swap, r.taken_heads.at[others]),
        (back_swap, r.seq_back.at[member]),
    ):
        await_bytes(region, r.small_send.at[kind])


def scatter_scratch(rows, width):
    half, quarter = rows // 2, rows // 4
    return (
        pltpu.VMEM((BLOCKS, rows, width), jnp.bfloat16),
        pltpu.VMEM((2, RING, 2, quarter, width), jnp.bfloat16),
        pltpu.VMEM((2, RING, 2, half, width), jnp.bfloat16),
        pltpu.VMEM((2, 2, quarter, width), jnp.bfloat16),
        pltpu.VMEM((2, 2, half, width), jnp.bfloat16),
    )


def body(
    prefill_x,
    span_index,
    prefix_pages,
    prefix_cache,
    decode_x,
    decode_len,
    page_order,
    assignment,
    kv_cache,
    w_query,
    w_keyval,
    w_out,
):
    span, depth = prefill_x.shape
    decode = decode_x.shape[1]
    rows = 2 * decode
    dec_dev = decode // SPLIT
    wide = w_query.shape[1]
    both = wide + w_keyval.shape[1]
    carried = wide + 2 * HEAD_DIM
    pre_rows = prefix_cache.shape[2]
    pool_pages = page_order.shape[2]
    exponent = np.arange(HEAD_DIM, dtype=np.float64) % (HEAD_DIM // 2) * (2.0 / HEAD_DIM)
    frequency = (rope_base ** (-exponent)).astype(np.float32)[None, :]
    hbm = pl.BlockSpec(memory_space=pl.ANY)
    operands = dict(
        pre_x=(prefill_x, hbm),
        dec_x=(decode_x.reshape(rows, depth), hbm),
        frequency_hbm=(jnp.asarray(frequency), hbm),
        span_index_hbm=(span_index, hbm),
        assignment_hbm=(assignment, hbm),
        prefix_pages_hbm=(prefix_pages, hbm),
        decode_len_hbm=(decode_len, hbm),
        page_order_hbm=(page_order, hbm),
        w_query=(w_query, hbm),
        w_keyval=(w_keyval, hbm),
        w_out=(w_out, hbm),
        prior_hbm=(prefix_cache.reshape(pre_rows, 2 * HEAD_DIM), hbm),
        pool_hbm=(kv_cache.reshape(pool_pages, PAGE, 2 * HEAD_DIM), hbm),
    )
    results = dict(
        pre_out=jax.ShapeDtypeStruct((span, depth), jnp.bfloat16),
        dec_out=jax.ShapeDtypeStruct((rows, depth), jnp.bfloat16),
    )
    narrow, full = jnp.bfloat16, jnp.float32
    scratch = dict(
        frequency=pltpu.VMEM((1, HEAD_DIM), full),
        span_index=pltpu.SMEM(span_index.shape, jnp.int32),
        assignment=pltpu.SMEM(assignment.shape, jnp.int32),
        prefix_pages=pltpu.SMEM(prefix_pages.shape, jnp.int32),
        decode_len=pltpu.SMEM(decode_len.shape, jnp.int32),
        page_order=pltpu.SMEM(page_order.shape, jnp.int32),
        pre_result=pltpu.VMEM((span, depth), narrow),
        dec_result=pltpu.VMEM((rows, depth), narrow),
        pre_held=pltpu.VMEM((BLOCKS, span, depth), narrow),
        dec_held=pltpu.VMEM((BLOCKS, rows, depth), narrow),
        weights=pltpu.VMEM((BLOCKS, depth, both), narrow),
        out_weights=pltpu.VMEM((BLOCKS, wide, depth), narrow),
        pre_total=pltpu.VMEM((span, both), full),
        dec_total=pltpu.VMEM((rows, both), full),
        pool=pltpu.VMEM((pool_pages, PAGE, 2 * HEAD_DIM), narrow),
        pages=pltpu.VMEM((pool_pages + MAX_PAGES, PAGE, 2 * HEAD_DIM), narrow),
        prior=pltpu.VMEM((pre_rows, 2 * HEAD_DIM), narrow),
        prior_bias=pltpu.VMEM((1, pre_rows), full),
        pre_cos=pltpu.VMEM((span, HEAD_DIM), full),
        pre_sin=pltpu.VMEM((span, HEAD_DIM), full),
        dec_cos=pltpu.VMEM((rows, HEAD_DIM), full),
        dec_sin=pltpu.VMEM((rows, HEAD_DIM), full),
        taken=pltpu.VMEM((rows, HEAD_DIM), full),
        picks=pltpu.VMEM((GROUPS * STEP_ROWS, rows), narrow),
        pre_pair=pltpu.VMEM((SPLIT, span, HEAD_DIM), narrow),
        dec_pair=pltpu.VMEM((SPLIT, rows, HEAD_DIM), narrow),
        pre_query=pltpu.VMEM((span, wide), narrow),
        pre_key=pltpu.VMEM((span, HEAD_DIM), narrow),
        pre_heads=pltpu.VMEM((span, wide), narrow),
        steps=pltpu.VMEM((rows, carried), narrow),
        seq_query=pltpu.VMEM((SPLIT, 2, dec_dev, wide), narrow),
        seq_rows=pltpu.VMEM((rows * wide // HEAD_DIM, HEAD_DIM), full),
        seq_key=pltpu.VMEM((2 * dec_dev, HEAD_DIM), full),
        seq_value=pltpu.VMEM((2 * dec_dev, HEAD_DIM), full),
        seq_out=pltpu.VMEM((rows * wide // HEAD_DIM, HEAD_DIM), full),
        seq_back=pltpu.VMEM((SPLIT, 2, dec_dev, wide), narrow),
        dec_heads=pltpu.VMEM((rows, wide), narrow),
        dec_final=pltpu.VMEM((rows, wide), narrow),
        visit_out=pltpu.VMEM((GROUPS * STEP_ROWS, carried), narrow),
        visit_in=pltpu.VMEM((GROUPS, STEP_ROWS, carried), narrow),
        taken_heads=pltpu.VMEM((GROUPS, STEP_ROWS, wide), narrow),
        **dict(zip(("pre_terms", "pre_relays", "pre_halves", "pre_relay2", "pre_halves2"), scatter_scratch(span, depth))),
        **dict(zip(("dec_terms", "dec_relays", "dec_halves", "dec_relay2", "dec_halves2"), scatter_scratch(rows, depth))),
        load=pltpu.SemaphoreType.DMA((BLOCKS,)),
        out_load=pltpu.SemaphoreType.DMA((BLOCKS,)),
        other_load=pltpu.SemaphoreType.DMA((12,)),
        send=pltpu.SemaphoreType.DMA((4,)),
        gather_receive=pltpu.SemaphoreType.DMA((2, 30)),
        scatter_receive=pltpu.SemaphoreType.DMA((2, 20)),
        small_send=pltpu.SemaphoreType.DMA((6,)),
        small_receive=pltpu.SemaphoreType.DMA((6,)),
    )
    names = tuple(operands) + tuple(results) + tuple(scratch)
    prefill_out, decode_out = pl.pallas_call(
        functools.partial(layer_kernel, names),
        out_shape=tuple(results.values()),
        in_specs=[spec for _, spec in operands.values()],
        out_specs=(hbm, hbm),
        scratch_shapes=list(scratch.values()),
        compiler_params=pltpu.CompilerParams(
            collective_id=0, has_side_effects=True, vmem_limit_bytes=60 * 2**20
        ),
        name="layer",
    )(*(value for value, _ in operands.values()))
    return (prefill_out, decode_out.reshape(2, decode, -1))


def solution(mesh):
    placed = (
        P("grp", "tp"),
        P(),
        P("grp", None),
        P("grp", "tp", None, None),
        P(None, "grp", "tp"),
        P("grp", None, None),
        P("grp", None, None),
        P(),
        P("grp", "tp", None, None),
        P(None, "tp"),
        P(None, "tp"),
        P("tp", None),
    )
    return jax.shard_map(
        body,
        mesh=mesh,
        in_specs=placed,
        out_specs=(P("grp", "tp"), P(None, "grp", "tp")),
        check_vma=False,
    )
```

```python
import functools
import types

import jax
import jax.numpy as jnp
import numpy as np
from jax import lax
from jax.experimental import pallas as pl
from jax.experimental.pallas import tpu as pltpu
from jax.sharding import PartitionSpec as P

KV_HEADS = 8
HEAD_DIM = 128
SPANS = 8
PAGE = 16
MAX_PAGES = 32
RING = 4
BLOCKS = RING * RING
SPLIT = 2
GROUPS = 8
STEP_ROWS = 16
MESH = pl.DeviceIdType.MESH

rope_base = 500000.0
masked_score = -1e30


def place(dz, dx):
    return (dz % RING) * RING + dx % RING


def neighbours():
    me = lax.axis_index("tp")
    z = me // RING
    x = me % RING
    return {
        ("z", 1): ((z + 1) % RING) * RING + x,
        ("z", -1): ((z + RING - 1) % RING) * RING + x,
        ("x", 1): z * RING + (x + 1) % RING,
        ("x", -1): z * RING + (x + RING - 1) % RING,
    }


def absolute(dz, dx):
    me = lax.axis_index("tp")
    z = me // RING
    x = me % RING
    return ((z + dz) % RING) * RING + (x + dx) % RING


def axes_of(half, first):
    return ("x", "z") if (half == 0) == first else ("z", "x")


def await_bytes(region, semaphore):
    pltpu.make_async_copy(region, region, semaphore).wait()


class Copies:
    def __init__(self, near, send, receive):
        self.near, self.send, self.receive = near, send, receive
        self.index = {}

    def start(self, name, axis, step, source, target):
        index = self.index.setdefault(name, len(self.index))
        pltpu.make_async_remote_copy(
            src_ref=source,
            dst_ref=target,
            send_sem=self.send,
            recv_sem=self.receive.at[index],
            device_id={"tp": self.near[axis, step]},
            device_id_type=MESH,
        ).start()

    def arrive(self, name, region):
        await_bytes(region, self.receive.at[self.index[name]])

    def sent(self, region):
        await_bytes(region, self.send)


class Gather:
    def __init__(self, own, held, copies):
        self.own, self.held, self.copies = own, held, copies
        self.rows = own.shape[0]

    def slot(self, half, d1, d2):
        return place(d2, d1) if half == 0 else place(d1, d2)

    def part(self, half, d1, d2, quarter=None):
        count = self.rows // 2
        first = half * count
        if quarter is not None:
            count = count // 2
            first = first + quarter * count
        return self.held.at[self.slot(half, d1, d2), pl.ds(first, count)]

    def mine(self, half):
        count = self.rows // 2
        return self.held.at[0, pl.ds(half * count, count)]

    def first_sends(self):
        for half in (0, 1):
            axis = axes_of(half, True)[0]
            for step in (1, -1):
                self.copies.start(
                    ("1", half, step), axis, step, self.mine(half), self.part(half, -step, 0)
                )
        self.second_sends(0)

    def second_sends(self, d1):
        for half in (0, 1):
            self.second_send(half, d1)

    def second_send(self, half, d1):
        axis = axes_of(half, True)[1]
        for step in (1, -1):
            self.copies.start(
                ("2", half, d1, step),
                axis,
                step,
                self.part(half, d1, 0) if d1 != 0 else self.mine(half),
                self.part(half, d1, -step),
            )

    def near_arrive(self):
        for half in (0, 1):
            axis = axes_of(half, True)[0]
            for step in (1, -1):
                quarter = 0 if step == 1 else 1
                self.copies.arrive(("1", half, step), self.part(half, -step, 0))
                self.copies.start(
                    ("1f", half),
                    axis,
                    step,
                    self.part(half, -step, 0, quarter),
                    self.part(half, -2 * step, 0, quarter),
                )
                self.second_send(half, -step)
        return [(half, d1, 0) for half in (0, 1) for d1 in (-1, 1)]

    def far_arrive(self):
        for half in (0, 1):
            self.copies.arrive(("1f", half), self.part(half, 2, 0))
            self.second_send(half, 2)
        return [(half, 2, 0) for half in (0, 1)]

    def line_arrive(self, d1):
        for half in (0, 1):
            axis = axes_of(half, True)[1]
            for step in (1, -1):
                quarter = 0 if step == 1 else 1
                self.copies.arrive(("2", half, d1, step), self.part(half, d1, -step))
                self.copies.start(
                    ("2f", half, d1),
                    axis,
                    step,
                    self.part(half, d1, -step, quarter),
                    self.part(half, d1, -2 * step, quarter),
                )
        return [(half, d1, d2) for half in (0, 1) for d2 in (-1, 1)]

    def last_arrive(self, d1):
        for half in (0, 1):
            self.copies.arrive(("2f", half, d1), self.part(half, d1, 2))
        return [(half, d1, 2) for half in (0, 1)]


class Scatter:
    def __init__(self, terms, relays, halves, relay2, halves2, out, copies):
        self.terms, self.relays, self.halves = terms, relays, halves
        self.relay2, self.halves2, self.out, self.copies = relay2, halves2, out, copies
        self.rows = terms.shape[1]

    def part(self, half, df, ds, quarter=None):
        count = self.rows // 2
        first = half * count
        if quarter is not None:
            count = count // 2
            first = first + quarter * count
        slot = place(df, ds) if half == 0 else place(ds, df)
        return self.terms.at[slot, pl.ds(first, count)]

    def relay_send(self, ds):
        for half in (0, 1):
            axis = axes_of(half, False)[0]
            for quarter, step in ((0, 1), (1, -1)):
                self.copies.start(
                    ("1r", half, ds),
                    axis,
                    step,
                    self.part(half, 2, ds, quarter),
                    self.relays.at[half, ds % RING, quarter],
                )

    def near_send(self, ds):
        for half in (0, 1):
            axis = axes_of(half, False)[0]
            self.copies.arrive(("1r", half, ds), self.relays.at[half, ds % RING])
            for quarter, step in ((0, 1), (1, -1)):
                own = self.part(half, step, ds, quarter)
                added = self.relays[half, ds % RING, quarter].astype(jnp.float32)
                own[...] = (own[...].astype(jnp.float32) + added).astype(jnp.bfloat16)
                self.copies.start(
                    ("1", half, ds),
                    axis,
                    step,
                    self.part(half, step, ds),
                    self.halves.at[half, ds % RING, quarter],
                )

    def line_sum(self, ds):
        for half in (0, 1):
            self.copies.arrive(("1", half, ds), self.halves.at[half, ds % RING])
            own = self.part(half, 0, ds)
            total = own[...].astype(jnp.float32)
            for side in (0, 1):
                total = total + self.halves[half, ds % RING, side].astype(jnp.float32)
            own[...] = total.astype(jnp.bfloat16)

    def relay_send2(self):
        for half in (0, 1):
            axis = axes_of(half, False)[1]
            for quarter, step in ((0, 1), (1, -1)):
                self.copies.start(
                    ("2r", half),
                    axis,
                    step,
                    self.part(half, 0, 2, quarter),
                    self.relay2.at[half, quarter],
                )

    def near_send2(self):
        for half in (0, 1):
            axis = axes_of(half, False)[1]
            self.copies.arrive(("2r", half), self.relay2.at[half])
            for quarter, step in ((0, 1), (1, -1)):
                own = self.part(half, 0, step, quarter)
                added = self.relay2[half, quarter].astype(jnp.float32)
                own[...] = (own[...].astype(jnp.float32) + added).astype(jnp.bfloat16)
                self.copies.start(
                    ("2", half),
                    axis,
                    step,
                    self.part(half, 0, step),
                    self.halves2.at[half, quarter],
                )

    def finish(self):
        count = self.rows // 2
        for half in (0, 1):
            self.copies.arrive(("2", half), self.halves2.at[half])
            total = self.part(half, 0, 0)[...].astype(jnp.float32)
            for side in (0, 1):
                total = total + self.halves2[half, side].astype(jnp.float32)
            self.out[pl.ds(half * count, count)] = total.astype(jnp.bfloat16)


def partner():
    me = lax.axis_index("tp")
    return me + 1 - 2 * (me % SPLIT)


def greet_all(near):
    barrier = pltpu.get_barrier_semaphore()
    group = lax.axis_index("grp")
    for device in near.values():
        pl.semaphore_signal(barrier, inc=1, device_id={"tp": device}, device_id_type=MESH)
    for step in range(1, GROUPS):
        other = (group + step) % GROUPS
        pl.semaphore_signal(barrier, inc=1, device_id={"grp": other}, device_id_type=MESH)
    pl.semaphore_wait(barrier, len(near) + GROUPS - 1)


ORDER = (
    ((2, 2),),
    ((2, -1), (-1, 2)),
    ((2, 1), (1, 2)),
    ((2, 0), (0, 2)),
    ((-1, -1), (-1, 1), (1, -1), (1, 1)),
    ((-1, 0), (1, 0), (0, -1), (0, 1)),
    ((0, 0),),
)


def lane_turn(values):
    half = HEAD_DIM // 2
    return jnp.concatenate([values[:, half:], values[:, :half]], 1)


def turn_tables(positions, frequency):
    angles = positions * frequency
    lanes = lax.broadcasted_iota(jnp.int32, angles.shape, 1)
    sine = jnp.sin(angles)
    return jnp.cos(angles), jnp.where(lanes < HEAD_DIM // 2, -sine, sine)


def turn(values, cosine, sine):
    return (values * cosine + lane_turn(values) * sine).astype(jnp.bfloat16)


def dot_rows(left, right):
    return lax.dot_general(
        left, right, (((1,), (1,)), ((), ())), preferred_element_type=jnp.float32
    )


def dot(left, right):
    return jnp.dot(left, right, preferred_element_type=jnp.float32)


def layer_kernel(names, *refs):
    r = types.SimpleNamespace(**dict(zip(names, refs)))
    near = neighbours()
    me = lax.axis_index("tp")
    group = lax.axis_index("grp")
    member = me % SPLIT
    pre_x, dec_x = r.pre_x, r.dec_x
    span, depth = pre_x.shape
    rows = dec_x.shape[0]
    decode = rows // 2
    dec_dev = decode // SPLIT
    wide = r.w_query.shape[1]
    heads_dev = wide // HEAD_DIM
    pre_rows = r.prior_hbm.shape[0]
    pool_pages = r.pool_hbm.shape[0]
    scale = HEAD_DIM ** (-0.5)

    loads, out_loads = {}, {}
    order = ((0, 0), (0, -1), (0, 1), (-1, 0), (1, 0), (0, 2), (2, 0), (-1, -1), (-1, 1), (1, -1))
    order += ((1, 1), (2, -1), (2, 1), (-1, 2), (1, 2), (2, 2))
    order = [place(*offset) for offset in order]
    weights, out_weights = r.weights, r.out_weights
    for slot in order:
        origin = absolute(slot // RING, slot % RING)
        span_rows = pl.ds(pl.multiple_of(origin * depth, depth), depth)
        loads[slot] = (
            pltpu.make_async_copy(
                r.w_query.at[span_rows],
                weights.at[slot, :, pl.ds(0, wide)],
                r.load.at[slot],
            ),
            pltpu.make_async_copy(
                r.w_keyval.at[span_rows],
                weights.at[slot, :, pl.ds(wide, HEAD_DIM)],
                r.load.at[slot],
            ),
        )
    for slot in order:
        origin = absolute(slot // RING, slot % RING)
        columns = pl.ds(pl.multiple_of(origin * depth, depth), depth)
        out_loads[slot] = pltpu.make_async_copy(
            r.w_out.at[:, columns], out_weights.at[slot], r.out_load.at[slot]
        )
    prior_load = pltpu.make_async_copy(r.prior_hbm, r.prior, r.other_load.at[0])
    pre_load = pltpu.make_async_copy(pre_x, r.pre_held.at[0], r.other_load.at[1])
    dec_load = pltpu.make_async_copy(dec_x, r.dec_held.at[0], r.other_load.at[2])
    pool_loads = []
    for part in range(4):
        pages = pl.ds(part * pool_pages // 4, pool_pages // 4)
        pool_loads.append(
            pltpu.make_async_copy(r.pool_hbm.at[pages], r.pool.at[pages], r.other_load.at[3])
        )
    small_loads = [
        pltpu.make_async_copy(source, target, r.other_load.at[4 + index])
        for index, (source, target) in enumerate(
            (
                (r.span_index_hbm, r.span_index),
                (r.assignment_hbm, r.assignment),
                (r.frequency_hbm, r.frequency),
                (r.prefix_pages_hbm, r.prefix_pages),
                (r.decode_len_hbm, r.decode_len),
                (r.page_order_hbm, r.page_order),
            )
        )
    ]
    pre_load.start()
    dec_load.start()
    for copy in small_loads:
        copy.start()
    for slot in order[:1]:
        for copy in loads[slot]:
            copy.start()
    waiting = [copy for slot in order[1:] for copy in loads[slot]]
    waiting += pool_loads + [prior_load] + [out_loads[place(*d)] for d in sum(ORDER, ())]

    def load_more(count):
        for copy in waiting[:count]:
            copy.start()
        del waiting[:count]

    greet_all(near)
    loaded = set()

    def multiply(gather, total, parts):
        for half, d1, d2 in parts:
            slot = gather.slot(half, d1, d2)
            if slot not in loaded:
                loaded.add(slot)
                await_bytes(weights.at[slot], r.load.at[slot])
            count = gather.rows // 2
            at = pl.ds(half * count, count)
            product = dot(gather.part(half, d1, d2)[...], weights[slot])
            if slot == 0:
                total[at] = product
            else:
                total[at] += product

    pre = Gather(pre_x, r.pre_held, Copies(near, r.send.at[0], r.gather_receive.at[0]))
    dec = Gather(dec_x, r.dec_held, Copies(near, r.send.at[1], r.gather_receive.at[1]))
    pre_total, dec_total = r.pre_total, r.dec_total
    pre_load.wait()
    pre.first_sends()
    load_more(12)
    multiply(pre, pre_total, [(0, 0, 0), (1, 0, 0)])

    for copy in small_loads:
        copy.wait()

    span_of = [r.span_index[s] for s in range(GROUPS)]
    goes_to = [r.assignment[s] for s in range(GROUPS)]
    to_here, owner = [], []
    rank = 0 * group
    for s in range(GROUPS):
        here = jnp.where((span_of[s] == SPANS - 1) & (goes_to[s] == group), 1, 0)
        to_here.append(here)
        owner.append((rank & 1) * dec_dev + (rank >> 1))
        rank = rank + here
    start_row = r.span_index[group] * span
    frequency = r.frequency[...]

    def prior_mask():
        live_pages = start_row // PAGE
        column_page = lax.broadcasted_iota(jnp.int32, (1, pre_rows), 1) // PAGE

        def mark(index, live):
            page = r.prefix_pages[0, index]
            page = jnp.where(index < live_pages, page, -1)
            return jnp.where(column_page == page, 0.0, live)

        live = jnp.full((1, pre_rows), masked_score, jnp.float32)
        r.prior_bias[...] = lax.fori_loop(0, pre_rows // PAGE, mark, live, unroll=8)

    def pre_tables():
        spots = (start_row + lax.broadcasted_iota(jnp.int32, (span, HEAD_DIM), 0)).astype(
            jnp.float32
        )
        cosine, sine = turn_tables(spots, frequency)
        r.pre_cos[...] = cosine
        r.pre_sin[...] = sine

    def dec_tables():
        row = lax.broadcasted_iota(jnp.int32, (rows, HEAD_DIM), 0)
        sequence = row % decode

        def spread(index, base):
            length = r.decode_len[0, index // dec_dev, index % dec_dev]
            return jnp.where(sequence == index, length, base)

        base = lax.fori_loop(0, decode, spread, jnp.zeros_like(row), unroll=4)
        taken = jnp.zeros(row.shape, jnp.float32)
        for s in range(GROUPS):
            mine = jnp.where(to_here[s] == 1, owner[s], -1)
            taken = jnp.where(sequence == mine, 1.0, taken)
        base = jnp.where(taken > 0.5, pre_rows + span, base)
        cosine, sine = turn_tables((base + row // decode).astype(jnp.float32), frequency)
        r.dec_cos[...] = cosine
        r.dec_sin[...] = sine
        r.taken[...] = taken
        row = lax.broadcasted_iota(jnp.int32, (STEP_ROWS, rows), 0)
        column = lax.broadcasted_iota(jnp.int32, (STEP_ROWS, rows), 1)
        for s in range(GROUPS):
            mine = jnp.where(to_here[s] == 1, owner[s], -rows)
            picked = (column == row * decode + mine) & (row < 2)
            r.picks[pl.ds(s * STEP_ROWS, STEP_ROWS)] = jnp.where(picked, 1.0, 0.0).astype(
                jnp.bfloat16
            )

    pieces = 8
    chunk = pool_pages // pieces

    def reorder(piece):
        def move(index, carry):
            page = r.page_order[0, member, index]
            r.pages[index] = r.pool[page]
            return carry

        lax.fori_loop(piece * chunk, (piece + 1) * chunk, move, 0, unroll=4)

    pre_tables()
    load_more(6)
    multiply(pre, pre_total, pre.near_arrive())
    prior_mask()
    load_more(6)
    multiply(pre, pre_total, pre.far_arrive())
    dec_tables()
    for d1 in (0, -1, 1, 2):
        parts = pre.line_arrive(d1)
        load_more(4)
        if d1 == 2:
            dec_load.wait()
            dec.first_sends()
        multiply(pre, pre_total, parts)
    multiply(dec, dec_total, [(0, 0, 0), (1, 0, 0)])
    await_bytes(r.pool, r.other_load.at[3])
    r.pages[pl.ds(pool_pages, MAX_PAGES)] = jnp.zeros(
        (MAX_PAGES, PAGE, 2 * HEAD_DIM), jnp.bfloat16
    )
    for index, d1 in enumerate((0, -1, 1, 2)):
        multiply(pre, pre_total, pre.last_arrive(d1))
        load_more(3)
        reorder(2 * index)
        reorder(2 * index + 1)
    load_more(len(waiting))

    def swap(kind, source, target, device):
        pltpu.make_async_remote_copy(
            src_ref=source,
            dst_ref=target,
            send_sem=r.small_send.at[kind],
            recv_sem=r.small_receive.at[kind],
            device_id=device,
            device_id_type=MESH,
        ).start()

    def swapped(kind, region):
        await_bytes(region, r.small_receive.at[kind])

    pre_swap, dec_swap, query_swap, visit_swap, take_swap, back_swap = range(6)
    others = pl.ds(1, GROUPS - 1)
    beside = {"tp": partner()}
    pre_pair, dec_pair = r.pre_pair, r.dec_pair
    pre_pair[member] = pre_total[:, wide:].astype(jnp.bfloat16)
    swap(pre_swap, pre_pair.at[member], pre_pair.at[member], beside)
    cosine, sine = r.pre_cos[...], r.pre_sin[...]
    for head in range(heads_dev):
        at = pl.ds(head * HEAD_DIM, HEAD_DIM)
        r.pre_query[:, at] = turn(pre_total[:, at], cosine, sine)
    dec_parts = dec.near_arrive()
    multiply(dec, dec_total, dec_parts)
    swapped(pre_swap, pre_pair.at[1 - member])
    r.pre_key[...] = turn(
        pre_pair[0].astype(jnp.float32), r.pre_cos[...], r.pre_sin[...]
    )
    prior_load.wait()
    prior_bias = r.prior_bias
    prior = r.prior
    block = span // 2

    def attend(head, part):
        at = pl.ds(head * HEAD_DIM, HEAD_DIM)
        here = pl.ds(part * block, block)
        query = r.pre_query[here, at]
        prior_scores = dot_rows(query, prior[:, pl.ds(0, HEAD_DIM)]) * scale + prior_bias[...]
        own_scores = dot_rows(query, r.pre_key[...]) * scale
        row = lax.broadcasted_iota(jnp.int32, own_scores.shape, 0) + part * block
        column = lax.broadcasted_iota(jnp.int32, own_scores.shape, 1)
        own_scores = jnp.where(row >= column, own_scores, masked_score)
        highest = jnp.maximum(
            jnp.max(prior_scores, 1, keepdims=True), jnp.max(own_scores, 1, keepdims=True)
        )
        prior_raised = jnp.exp(prior_scores - highest)
        own_raised = jnp.exp(own_scores - highest)
        total = jnp.sum(prior_raised, 1, keepdims=True) + jnp.sum(own_raised, 1, keepdims=True)
        values = dot(prior_raised.astype(jnp.bfloat16), prior[:, pl.ds(HEAD_DIM, HEAD_DIM)])
        values = values + dot(own_raised.astype(jnp.bfloat16), pre_pair[1])
        r.pre_heads[here, at] = (values / total).astype(jnp.bfloat16)

    def terms(heads, kept, blocks):
        for dz, dx in blocks:
            slot = place(dz, dx)
            if slot not in term_loaded:
                term_loaded.add(slot)
                out_loads[slot].wait()
            kept[slot] = dot(heads[...], out_weights[slot]).astype(jnp.bfloat16)

    term_loaded = set()
    pre_scatter = Scatter(
        r.pre_terms,
        r.pre_relays,
        r.pre_halves,
        r.pre_relay2,
        r.pre_halves2,
        r.pre_result,
        Copies(near, r.send.at[2], r.scatter_receive.at[0]),
    )
    dec_scatter = Scatter(
        r.dec_terms,
        r.dec_relays,
        r.dec_halves,
        r.dec_relay2,
        r.dec_halves2,
        r.dec_result,
        Copies(near, r.send.at[3], r.scatter_receive.at[1]),
    )
    pre_heads, pre_terms = r.pre_heads, r.pre_terms
    work = [(head, part) for head in range(heads_dev) for part in (0, 1)]
    events = [dec.far_arrive]
    events += [functools.partial(dec.line_arrive, d1) for d1 in (0, -1, 1, 2)]
    parts = []
    for index, item in enumerate(work):
        if index < len(events):
            parts += events[index]()
        attend(*item)
    parts += dec.last_arrive(0)
    parts += dec.last_arrive(-1)
    for index, ds in enumerate((2, -1)):
        terms(pre_heads, pre_terms, ORDER[index])
        pre_scatter.relay_send(ds)
    multiply(dec, dec_total, parts)
    for d1 in (1, 2):
        multiply(dec, dec_total, dec.last_arrive(d1))

    dec_pair[member] = dec_total[:, wide:].astype(jnp.bfloat16)
    swap(dec_swap, dec_pair.at[member], dec_pair.at[member], beside)
    cosine, sine = r.dec_cos[...], r.dec_sin[...]
    for head in range(heads_dev):
        at = pl.ds(head * HEAD_DIM, HEAD_DIM)
        r.steps[:, at] = turn(dec_total[:, at], cosine, sine)

    def of_member(t, which):
        return pl.ds(pl.multiple_of(t * decode + which * dec_dev, dec_dev), dec_dev)

    for t in (0, 1):
        swap(
            query_swap,
            r.steps.at[of_member(t, 1 - member), pl.ds(0, wide)],
            r.seq_query.at[member, t],
            beside,
        )
        r.seq_query[member, t] = r.steps[of_member(t, member), pl.ds(0, wide)]

    terms(pre_heads, pre_terms, ORDER[2])
    pre_scatter.relay_send(1)
    terms(pre_heads, pre_terms, ORDER[3])
    pre_scatter.relay_send(0)
    pre_scatter.near_send(2)
    terms(pre_heads, pre_terms, ORDER[4])

    swapped(dec_swap, dec_pair.at[1 - member])
    r.steps[:, pl.ds(wide, HEAD_DIM)] = turn(
        dec_pair[0].astype(jnp.float32), r.dec_cos[...], r.dec_sin[...]
    )
    r.steps[:, pl.ds(wide + HEAD_DIM, HEAD_DIM)] = dec_pair[1]
    r.visit_out[...] = dot(r.picks[...], r.steps[...]).astype(jnp.bfloat16)
    for step in range(1, GROUPS):
        other = (group + step) % GROUPS
        here = pl.ds(pl.multiple_of(other * STEP_ROWS, STEP_ROWS), STEP_ROWS)
        swap(visit_swap, r.visit_out.at[here], r.visit_in.at[step], {"grp": other})
    for t in (0, 1):
        here = pl.ds(t * dec_dev, dec_dev)
        r.seq_key[here] = r.steps[of_member(t, member), pl.ds(wide, HEAD_DIM)].astype(
            jnp.float32
        )
        r.seq_value[here] = r.steps[
            of_member(t, member), pl.ds(wide + HEAD_DIM, HEAD_DIM)
        ].astype(jnp.float32)
    pre_scatter.near_send(-1)
    swapped(query_swap, r.seq_query.at[1 - member])
    for head in range(heads_dev):
        lines = r.seq_query[:, :, :, pl.ds(head * HEAD_DIM, HEAD_DIM)]
        r.seq_rows[pl.ds(head * rows, rows)] = lines.reshape(rows, HEAD_DIM).astype(jnp.float32)

    counts = [
        (r.decode_len[0, member, index] + (PAGE - 1)) >> 4 for index in range(dec_dev)
    ]
    firsts, total_pages = [], 0
    for index in range(dec_dev):
        firsts.append(total_pages)
        total_pages = total_pages + counts[index]

    def cached_some(part):
        sequences = range(part * dec_dev // 8, (part + 1) * dec_dev // 8)
        lines = [pl.ds(index, 2 * SPLIT * heads_dev, stride=dec_dev) for index in sequences]
        pages = [pl.ds(firsts[index], MAX_PAGES) for index in sequences]
        found = []
        for at, index, here in zip(lines, sequences, pages):
            query = r.seq_rows[at, :]
            keys = r.pages[here, :, pl.ds(0, HEAD_DIM)].reshape(MAX_PAGES * PAGE, HEAD_DIM)
            scores = dot_rows(query.astype(jnp.bfloat16), keys) * scale
            column = lax.broadcasted_iota(jnp.int32, scores.shape, 1)
            scores = jnp.where(column < r.decode_len[0, member, index], scores, masked_score)
            step0 = jnp.sum(query * r.seq_key[pl.ds(index, 1)], 1, keepdims=True) * scale
            step1 = jnp.sum(query * r.seq_key[pl.ds(dec_dev + index, 1)], 1, keepdims=True) * scale
            found.append((scores, step0, step1))
        raised = []
        for scores, step0, step1 in found:
            second = lax.broadcasted_iota(jnp.int32, step1.shape, 0) % 2 == 1
            step1 = jnp.where(second, step1, masked_score)
            highest = jnp.maximum(jnp.max(scores, 1, keepdims=True), jnp.maximum(step0, step1))
            scores = jnp.exp(scores - highest)
            step0 = jnp.exp(step0 - highest)
            step1 = jnp.exp(step1 - highest)
            total = jnp.sum(scores, 1, keepdims=True) + step0 + step1
            raised.append((scores.astype(jnp.bfloat16), step0, step1, total))
        attended = []
        for here, (scores, step0, step1, total) in zip(pages, raised):
            values = r.pages[here, :, pl.ds(HEAD_DIM, HEAD_DIM)]
            attended.append(dot(scores, values.reshape(MAX_PAGES * PAGE, HEAD_DIM)))
        for at, index, values, (scores, step0, step1, total) in zip(
            lines, sequences, attended, raised
        ):
            values = values + step0 * r.seq_value[pl.ds(index, 1)]
            values = values + step1 * r.seq_value[pl.ds(dec_dev + index, 1)]
            r.seq_out[at, :] = values / total

    def visiting():
        swapped(visit_swap, r.visit_in.at[others])
        own = r.visit_out[pl.ds(pl.multiple_of(group * STEP_ROWS, STEP_ROWS), STEP_ROWS)]
        total = own.astype(jnp.float32)
        for step in range(1, GROUPS):
            total = total + r.visit_in[step].astype(jnp.float32)
        query = jnp.concatenate(
            [total[:, head * HEAD_DIM : (head + 1) * HEAD_DIM] for head in range(heads_dev)], 0
        ).astype(jnp.bfloat16)
        new_key = total[:, wide : wide + HEAD_DIM].astype(jnp.bfloat16)
        new_value = total[:, wide + HEAD_DIM :].astype(jnp.bfloat16)
        prior_scores = dot_rows(query, prior[:, pl.ds(0, HEAD_DIM)]) * scale + prior_bias[...]
        own_scores = dot_rows(query, r.pre_key[...]) * scale
        step_scores = dot_rows(query, new_key) * scale
        row = lax.broadcasted_iota(jnp.int32, step_scores.shape, 0) % STEP_ROWS
        column = lax.broadcasted_iota(jnp.int32, step_scores.shape, 1)
        step_scores = jnp.where((column <= row) & (column < 2), step_scores, masked_score)
        highest = jnp.maximum(
            jnp.max(prior_scores, 1, keepdims=True), jnp.max(own_scores, 1, keepdims=True)
        )
        highest = jnp.maximum(highest, jnp.max(step_scores, 1, keepdims=True))
        prior_raised = jnp.exp(prior_scores - highest)
        own_raised = jnp.exp(own_scores - highest)
        step_raised = jnp.exp(step_scores - highest)
        total = jnp.sum(prior_raised, 1, keepdims=True) + jnp.sum(own_raised, 1, keepdims=True)
        total = total + jnp.sum(step_raised, 1, keepdims=True)
        values = dot(prior_raised.astype(jnp.bfloat16), prior[:, pl.ds(HEAD_DIM, HEAD_DIM)])
        values = values + dot(own_raised.astype(jnp.bfloat16), pre_pair[1])
        values = values + dot(step_raised.astype(jnp.bfloat16), new_value)
        values = (values / total).astype(jnp.bfloat16)
        for head in range(heads_dev):
            r.taken_heads[group, :, pl.ds(head * HEAD_DIM, HEAD_DIM)] = values[
                head * STEP_ROWS : (head + 1) * STEP_ROWS
            ]
        for step in range(1, GROUPS):
            other = (group + step) % GROUPS
            swap(take_swap, r.taken_heads.at[group], r.taken_heads.at[group], {"grp": other})

    cached_some(0)
    pre_scatter.near_send(1)
    cached_some(1)
    terms(pre_heads, pre_terms, ORDER[5] + ORDER[6])
    cached_some(2)
    visiting()
    cached_some(3)
    pre_scatter.line_sum(2)
    pre_scatter.relay_send2()
    cached_some(4)
    cached_some(5)
    cached_some(6)
    cached_some(7)

    for head in range(heads_dev):
        lines = r.seq_out[pl.ds(head * rows, rows)].reshape(SPLIT, 2, dec_dev, HEAD_DIM)
        r.seq_back[:, :, :, pl.ds(head * HEAD_DIM, HEAD_DIM)] = lines.astype(jnp.bfloat16)
    dec_heads = r.dec_heads
    for t in (0, 1):
        swap(
            back_swap,
            r.seq_back.at[1 - member, t],
            dec_heads.at[of_member(t, member)],
            beside,
        )
        dec_heads[of_member(t, member)] = r.seq_back[member, t]
    pre_scatter.near_send(0)
    pre_scatter.line_sum(-1)
    pre_scatter.line_sum(1)
    pre_scatter.near_send2()
    swapped(take_swap, r.taken_heads.at[others])
    placed = lax.dot_general(
        r.picks[...],
        r.taken_heads[...].reshape(GROUPS * STEP_ROWS, wide),
        (((0,), (0,)), ((), ())),
        preferred_element_type=jnp.float32,
    )
    swapped(back_swap, r.seq_back.at[1 - member])
    taken = r.taken[:, 0:1] > 0.5
    r.dec_final[...] = jnp.where(taken, placed, dec_heads[...].astype(jnp.float32)).astype(
        jnp.bfloat16
    )
    dec_final, dec_terms = r.dec_final, r.dec_terms
    for index, ds in enumerate((2, -1, 1, 0)):
        terms(dec_final, dec_terms, ORDER[index])
        dec_scatter.relay_send(ds)
    dec_scatter.near_send(2)
    terms(dec_final, dec_terms, ORDER[4])
    dec_scatter.near_send(-1)
    dec_scatter.near_send(1)
    terms(dec_final, dec_terms, ORDER[5] + ORDER[6])
    pre_scatter.line_sum(0)
    pre_scatter.finish()
    pre_store = pltpu.make_async_copy(r.pre_result, r.pre_out, r.other_load.at[10])
    pre_store.start()
    dec_scatter.line_sum(2)
    dec_scatter.relay_send2()
    dec_scatter.near_send(0)
    dec_scatter.line_sum(-1)
    dec_scatter.line_sum(1)
    dec_scatter.near_send2()
    dec_scatter.line_sum(0)
    dec_scatter.finish()
    dec_store = pltpu.make_async_copy(r.dec_result, r.dec_out, r.other_load.at[11])
    dec_store.start()
    pre_store.wait()
    dec_store.wait()
    rest = pl.ds(1, BLOCKS - 1)
    pre.copies.sent(pre.held.at[rest])
    dec.copies.sent(dec.held.at[rest])
    pre_scatter.copies.sent(pre_terms.at[rest])
    dec_scatter.copies.sent(dec_terms.at[rest])
    for kind, region in (
        (pre_swap, pre_pair.at[member]),
        (dec_swap, dec_pair.at[member]),
        (query_swap, r.seq_query.at[member]),
        (visit_swap, r.visit_in.at[others]),
        (take_swap, r.taken_heads.at[others]),
        (back_swap, r.seq_back.at[member]),
    ):
        await_bytes(region, r.small_send.at[kind])


def results_kernel(pre_from, dec_from, pre_to, dec_to, pre_held, dec_held, done):
    moves = []
    for index, (source, held, target) in enumerate(
        ((pre_from, pre_held, pre_to), (dec_from, dec_held, dec_to))
    ):
        fetch = pltpu.make_async_copy(source, held, done.at[0, index])
        fetch.start()
        moves.append((fetch, pltpu.make_async_copy(held, target, done.at[1, index])))
    for fetch, store in moves:
        fetch.wait()
        store.start()
    for _, store in moves:
        store.wait()


def scatter_scratch(rows, width):
    half, quarter = rows // 2, rows // 4
    return (
        pltpu.VMEM((BLOCKS, rows, width), jnp.bfloat16),
        pltpu.VMEM((2, RING, 2, quarter, width), jnp.bfloat16),
        pltpu.VMEM((2, RING, 2, half, width), jnp.bfloat16),
        pltpu.VMEM((2, 2, quarter, width), jnp.bfloat16),
        pltpu.VMEM((2, 2, half, width), jnp.bfloat16),
    )


def body(
    prefill_x,
    span_index,
    prefix_pages,
    prefix_cache,
    decode_x,
    decode_len,
    page_order,
    assignment,
    kv_cache,
    w_query,
    w_keyval,
    w_out,
):
    span, depth = prefill_x.shape
    decode = decode_x.shape[1]
    rows = 2 * decode
    dec_dev = decode // SPLIT
    wide = w_query.shape[1]
    both = wide + w_keyval.shape[1]
    carried = wide + 2 * HEAD_DIM
    pre_rows = prefix_cache.shape[2]
    pool_pages = page_order.shape[2]
    exponent = np.arange(HEAD_DIM, dtype=np.float64) % (HEAD_DIM // 2) * (2.0 / HEAD_DIM)
    frequency = (rope_base ** (-exponent)).astype(np.float32)[None, :]
    hbm = pl.BlockSpec(memory_space=pl.ANY)
    operands = dict(
        pre_x=(prefill_x, hbm),
        dec_x=(decode_x.reshape(rows, depth), hbm),
        frequency_hbm=(jnp.asarray(frequency), hbm),
        span_index_hbm=(span_index, hbm),
        assignment_hbm=(assignment, hbm),
        prefix_pages_hbm=(prefix_pages, hbm),
        decode_len_hbm=(decode_len, hbm),
        page_order_hbm=(page_order, hbm),
        w_query=(w_query, hbm),
        w_keyval=(w_keyval, hbm),
        w_out=(w_out, hbm),
        prior_hbm=(prefix_cache.reshape(pre_rows, 2 * HEAD_DIM), hbm),
        pool_hbm=(kv_cache.reshape(pool_pages, PAGE, 2 * HEAD_DIM), hbm),
    )
    results = dict(
        pre_out=jax.ShapeDtypeStruct((span, depth), jnp.bfloat16),
        dec_out=jax.ShapeDtypeStruct((rows, depth), jnp.bfloat16),
    )
    narrow, full = jnp.bfloat16, jnp.float32
    scratch = dict(
        frequency=pltpu.VMEM((1, HEAD_DIM), full),
        span_index=pltpu.SMEM(span_index.shape, jnp.int32),
        assignment=pltpu.SMEM(assignment.shape, jnp.int32),
        prefix_pages=pltpu.SMEM(prefix_pages.shape, jnp.int32),
        decode_len=pltpu.SMEM(decode_len.shape, jnp.int32),
        page_order=pltpu.SMEM(page_order.shape, jnp.int32),
        pre_result=pltpu.VMEM((span, depth), narrow),
        dec_result=pltpu.VMEM((rows, depth), narrow),
        pre_held=pltpu.VMEM((BLOCKS, span, depth), narrow),
        dec_held=pltpu.VMEM((BLOCKS, rows, depth), narrow),
        weights=pltpu.VMEM((BLOCKS, depth, both), narrow),
        out_weights=pltpu.VMEM((BLOCKS, wide, depth), narrow),
        pre_total=pltpu.VMEM((span, both), full),
        dec_total=pltpu.VMEM((rows, both), full),
        pool=pltpu.VMEM((pool_pages, PAGE, 2 * HEAD_DIM), narrow),
        pages=pltpu.VMEM((pool_pages + MAX_PAGES, PAGE, 2 * HEAD_DIM), narrow),
        prior=pltpu.VMEM((pre_rows, 2 * HEAD_DIM), narrow),
        prior_bias=pltpu.VMEM((1, pre_rows), full),
        pre_cos=pltpu.VMEM((span, HEAD_DIM), full),
        pre_sin=pltpu.VMEM((span, HEAD_DIM), full),
        dec_cos=pltpu.VMEM((rows, HEAD_DIM), full),
        dec_sin=pltpu.VMEM((rows, HEAD_DIM), full),
        taken=pltpu.VMEM((rows, HEAD_DIM), full),
        picks=pltpu.VMEM((GROUPS * STEP_ROWS, rows), narrow),
        pre_pair=pltpu.VMEM((SPLIT, span, HEAD_DIM), narrow),
        dec_pair=pltpu.VMEM((SPLIT, rows, HEAD_DIM), narrow),
        pre_query=pltpu.VMEM((span, wide), narrow),
        pre_key=pltpu.VMEM((span, HEAD_DIM), narrow),
        pre_heads=pltpu.VMEM((span, wide), narrow),
        steps=pltpu.VMEM((rows, carried), narrow),
        seq_query=pltpu.VMEM((SPLIT, 2, dec_dev, wide), narrow),
        seq_rows=pltpu.VMEM((rows * wide // HEAD_DIM, HEAD_DIM), full),
        seq_key=pltpu.VMEM((2 * dec_dev, HEAD_DIM), full),
        seq_value=pltpu.VMEM((2 * dec_dev, HEAD_DIM), full),
        seq_out=pltpu.VMEM((rows * wide // HEAD_DIM, HEAD_DIM), full),
        seq_back=pltpu.VMEM((SPLIT, 2, dec_dev, wide), narrow),
        dec_heads=pltpu.VMEM((rows, wide), narrow),
        dec_final=pltpu.VMEM((rows, wide), narrow),
        visit_out=pltpu.VMEM((GROUPS * STEP_ROWS, carried), narrow),
        visit_in=pltpu.VMEM((GROUPS, STEP_ROWS, carried), narrow),
        taken_heads=pltpu.VMEM((GROUPS, STEP_ROWS, wide), narrow),
        **dict(zip(("pre_terms", "pre_relays", "pre_halves", "pre_relay2", "pre_halves2"), scatter_scratch(span, depth))),
        **dict(zip(("dec_terms", "dec_relays", "dec_halves", "dec_relay2", "dec_halves2"), scatter_scratch(rows, depth))),
        load=pltpu.SemaphoreType.DMA((BLOCKS,)),
        out_load=pltpu.SemaphoreType.DMA((BLOCKS,)),
        other_load=pltpu.SemaphoreType.DMA((12,)),
        send=pltpu.SemaphoreType.DMA((4,)),
        gather_receive=pltpu.SemaphoreType.DMA((2, 30)),
        scatter_receive=pltpu.SemaphoreType.DMA((2, 20)),
        small_send=pltpu.SemaphoreType.DMA((6,)),
        small_receive=pltpu.SemaphoreType.DMA((6,)),
    )
    names = tuple(operands) + tuple(results) + tuple(scratch)
    prefill_out, decode_out = pl.pallas_call(
        functools.partial(layer_kernel, names),
        out_shape=tuple(results.values()),
        in_specs=[spec for _, spec in operands.values()],
        out_specs=(hbm, hbm),
        scratch_shapes=list(scratch.values()),
        compiler_params=pltpu.CompilerParams(
            collective_id=0, has_side_effects=True, vmem_limit_bytes=60 * 2**20
        ),
        name="layer",
    )(*(value for value, _ in operands.values()))
    prefill_out, decode_out = pl.pallas_call(
        results_kernel,
        out_shape=tuple(results.values()),
        in_specs=[hbm, hbm],
        out_specs=(hbm, hbm),
        scratch_shapes=[
            pltpu.VMEM((span, depth), narrow),
            pltpu.VMEM((rows, depth), narrow),
            pltpu.SemaphoreType.DMA((2, 2)),
        ],
        name="results",
    )(prefill_out, decode_out)
    return (prefill_out, decode_out.reshape(2, decode, -1))


def solution(mesh):
    placed = (
        P("grp", "tp"),
        P(),
        P("grp", None),
        P("grp", "tp", None, None),
        P(None, "grp", "tp"),
        P("grp", None, None),
        P("grp", None, None),
        P(),
        P("grp", "tp", None, None),
        P(None, "tp"),
        P(None, "tp"),
        P("tp", None),
    )
    return jax.shard_map(
        body,
        mesh=mesh,
        in_specs=placed,
        out_specs=(P("grp", "tp"), P(None, "grp", "tp")),
        check_vma=False,
    )
```
